32 devices in a mesh: grp: 2 (over y), row: 8 (over z, x), col: 2 (over core).
Axes of the slice: x: 2, y: 2, z: 4, core: 2. Of those that a mesh axis runs over, the one named last changes fastest.
Arguments:
- acts: bfloat16 [32, 8192], P(('grp', 'row'), 'col'), parts along dimension 0, may hold values from -6 to 6
- grads: bfloat16 [32, 10240], P(('grp', 'row'), 'col'), parts along dimension 0, may hold values from -6 to 6
- eigen_a: bfloat16 [2, 4096, 8192], P('col', 'row'), may hold values from -0.0625 to 0.0625
- eigen_s_rows: bfloat16 [10240, 10240], P('row', 'col'), may hold values from -0.0625 to 0.0625
- doc_lengths: int32 [24], P('grp'), parts along dimension 0, may hold values from 1 to 4, 16 in all
- doc_plan: int32 [24], P('grp'), parts along dimension 0, may hold values from 0 to 5, as said below
Outputs:
- correction: float32 [20480, 8192], P(('grp', 'row'), 'col'), parts along dimension 0
The draws below stay inside these ranges and needn't reach their ends.
There are 2 independent parts, one for each index of `grp`. The reference program is written for one: setup_inputs(seed, part) draws one part's arguments, and reference() takes and returns one part's arrays. A program takes and returns all parts, laid end to end along the dimension named above; an argument that names none is the same for every part. Nothing has to cross between parts.
Inputs may be any that keep to these rules, and one draw needn't show every extreme that they name: `doc_plan`: every one of the 6 sequences receives at least one document.
All inputs are finite; a program needn't handle non-finite values.
Results may differ from the reference program's by a relative error of at most 0.006.
Values may be sent and summed in bfloat16 or wider, within the bound.
No kernel may reach another device: no remote copies, remote signals or barrier semaphores. Data moves between devices by JAX's collectives and lax.ppermute only.
A program may use at most 128 MiB of HBM per device.

```python
import math
import jax
import jax.numpy as jnp
import numpy as np

D_IN = 8192
D_OUT = 10240
DOCS = 12
N_SEQ = 6
TOKENS = 16
MOST = 4
N_COL = 2


def draw_doc_plan(key, part):
    key = jax.random.fold_in(key, 7)
    key_first, key_second, key_third = jax.random.split(key, 3)
    covered = jax.random.permutation(key_first, N_SEQ).astype(jnp.int32)
    extra = jax.random.randint(key_second, (DOCS - N_SEQ,), 0, N_SEQ).astype(jnp.int32)
    joined = jnp.concatenate([covered, extra])
    shuffle_order = jax.random.permutation(key_third, DOCS)
    return joined[shuffle_order].astype(jnp.int32)


def level_of(rng, shape, cuts, least, high):
    factor_of, own = 1.0, jax.random.fold_in(rng, 6)
    for dim, blocks in cuts:
        heights = jnp.exp(jax.random.uniform(jax.random.fold_in(own, dim), (blocks,), jnp.float32, least / len(cuts), high / len(cuts)))
        factor_of = factor_of * jnp.repeat(heights, shape[dim] // blocks).reshape([-1 if axis == dim else 1 for axis in range(len(shape))])
    return factor_of


def split_up(amount, total, bound, skew):
    loads = [(1 << 20) // math.isqrt(rank ** skew) + 1 for rank in range(2, amount + 1)]
    rest, counts = total - bound - (amount - 1), [1] * (amount - 1)
    while rest > 0:
        candidates = [i for i in range(amount - 1) if counts[i] < bound]
        whole, remaining = sum([loads[i] for i in candidates]), rest
        for i in candidates:
            more = min(bound - counts[i], max(1, remaining * loads[i] // whole), rest)
            counts[i] = counts[i] + more
            rest = rest - more
    return np.array([bound] + counts)


def uneven_parts(key, amount, total, most, lean):
    if amount == 2:
        one = jax.random.randint(key, (), max(1, total - most), min(most, total - 1) + 1)
        return jnp.stack([one, total - one])
    lengths = jnp.asarray(split_up(amount, total, most, lean), jnp.int32)
    pairs = (amount - 1) // 2
    giver, taker = lengths[1:1 + 2 * pairs:2], lengths[2:2 + 2 * pairs:2]
    slack = jnp.minimum(giver - 1, most - taker)
    shifted = jax.random.randint(jax.random.fold_in(key, 1), (pairs,), 0, 1 << 20) % (slack + 1)
    lengths = lengths.at[1:1 + 2 * pairs:2].set(giver - shifted).at[2:2 + 2 * pairs:2].set(taker + shifted)
    return lengths[jax.random.permutation(jax.random.fold_in(key, 2), amount)]


def gaussian(own_key, shape, scale, limit, cuts=(), held_as=jnp.bfloat16):
    loudness = level_of(own_key, shape, cuts, -0.22, 0.18) if cuts else 1.0
    values = jax.random.normal(own_key, shape, jnp.float32) * scale * loudness
    return jnp.minimum(jnp.maximum(values, -limit), limit).astype(held_as)


def setup_inputs(seed: int = 0, part: int = 0) -> dict:
    key_of = jax.random.split(jax.random.key(seed), 7)
    part_keys = jax.random.split(jax.random.fold_in(key_of[6], part), 7)
    acts = gaussian(part_keys[0], (TOKENS, D_IN), 1.0, 6.0, ((0, 8), (1, 2)))
    grads = gaussian(part_keys[1], (TOKENS, D_OUT), 1.0, 6.0, ((0, 8), (1, 2)))
    eigen_a = gaussian(key_of[2], (N_COL, D_IN // N_COL, D_IN), D_IN ** -0.5, 0.0625, ((0, 2), (1, 8)))
    eigen_s_rows = gaussian(key_of[3], (D_OUT, D_OUT), D_OUT ** -0.5, 0.0625, ((0, 8), (1, 2)))
    doc_lengths = uneven_parts(part_keys[4], DOCS, TOKENS, MOST, 2).astype(jnp.int32)
    doc_plan = draw_doc_plan(jax.random.fold_in(jax.random.fold_in(key_of[6], part), 71), part)
    return {"acts": acts, "grads": grads, "eigen_a": eigen_a, "eigen_s_rows": eigen_s_rows, "doc_lengths": doc_lengths, "doc_plan": doc_plan}


def sequence_index(doc_lengths, doc_plan, total_tokens):
    positions = jnp.arange(total_tokens, dtype=jnp.int32)
    doc_ends = jnp.cumsum(doc_lengths).astype(jnp.int32)
    doc_index = jnp.sum((positions[:, None] >= doc_ends[None, :]).astype(jnp.int32), axis=1)
    doc_onehot = (doc_index[:, None] == jnp.arange(doc_lengths.shape[0], dtype=jnp.int32)[None, :]).astype(jnp.int32)
    return jnp.sum(doc_onehot * doc_plan[None, :], axis=1).astype(jnp.int32)


def reference(acts, grads, eigen_a, eigen_s_rows, doc_lengths, doc_plan):
    basis_a = eigen_a.reshape(D_IN, D_IN)
    a_rot = jnp.dot(acts, basis_a.T, preferred_element_type=jnp.float32).astype(jnp.bfloat16)
    g_rot = jnp.dot(grads, eigen_s_rows.T, preferred_element_type=jnp.float32).astype(jnp.bfloat16)
    seq_index = sequence_index(doc_lengths, doc_plan, TOKENS)
    correction = jnp.zeros((D_OUT, D_IN), jnp.float32)
    for sequence in range(N_SEQ):
        seq_mask = (seq_index == sequence).astype(jnp.bfloat16)
        masked = g_rot * seq_mask[:, None]
        grad_tile = jnp.dot(masked.T, a_rot, preferred_element_type=jnp.float32)
        correction = correction + grad_tile * grad_tile
    return correction / TOKENS
```

```python
import functools
import jax
import jax.numpy as jnp
from jax import lax
from jax.experimental import pallas as pl
from jax.experimental.pallas import tpu as pltpu
from jax.sharding import PartitionSpec as P

N_SEQ = 6
PAIR_ROWS = 80
BF16 = jnp.bfloat16
F32 = jnp.float32
I32 = jnp.int32
NT = (((1,), (1,)), ((), ()))
VMEM_LIMIT = 50 * 1024 * 1024


def iota(shape, dim):
    return lax.broadcasted_iota(I32, shape, dim)


def dot(a, b, dims=(((1,), (0,)), ((), ()))):
    return lax.dot_general(a, b, dims, preferred_element_type=F32)


def sequence_index(doc_lengths, doc_plan, total_tokens):
    positions = jnp.arange(total_tokens, dtype=I32)
    doc_ends = jnp.cumsum(doc_lengths)
    doc_index = jnp.sum((positions[:, None] >= doc_ends[None, :]).astype(I32), axis=1)
    doc_onehot = (doc_index[:, None] == jnp.arange(doc_lengths.shape[0], dtype=I32)[None, :]).astype(I32)
    return jnp.sum(doc_onehot * doc_plan[None, :], axis=1)


def general_body(acts, grads, eigen_a, eigen_s_rows, doc_lengths, doc_plan):
    act_rows = lax.all_gather(acts, "row", axis=0, tiled=True)
    act_full = lax.all_gather(act_rows, "col", axis=1, tiled=True)
    a_block = dot(eigen_a[0], act_full, NT).astype(BF16)
    a_rot = lax.all_gather(a_block, "row", axis=0, tiled=True)
    grad_terms = dot(eigen_s_rows, lax.all_gather(grads, "row", axis=0, tiled=True), NT)
    g_rot = lax.psum(grad_terms, "col").astype(BF16)
    total_tokens = g_rot.shape[1]
    seq_index = sequence_index(doc_lengths, doc_plan, total_tokens)
    correction = jnp.zeros((g_rot.shape[0], a_rot.shape[0]), F32)
    for sequence in range(N_SEQ):
        inside = (seq_index == sequence).astype(BF16)
        term = dot(g_rot * inside[None, :], a_rot, NT)
        correction = correction + term * term
    return correction / total_tokens


def pairs_kernel(row_ref, len_ref, plan_ref, s1a_ref, s2a_ref, s1g_ref, s2g_ref, perm_ref):
    docs = len_ref.shape[1]
    tokens = perm_ref.shape[0]
    grid_pairs = tokens * tokens
    me = row_ref[0]
    upper = (iota((docs, docs), 0) <= iota((docs, docs), 1)).astype(F32)
    ends = dot(jnp.broadcast_to(len_ref[...].astype(F32), (8, docs)), upper)[0:1]
    position = iota((tokens, docs), 0).astype(F32)
    doc = jnp.sum((ends <= position).astype(F32), axis=1, keepdims=True)
    onehot = doc == iota((tokens, docs), 1).astype(F32)
    seq = jnp.sum(jnp.where(onehot, plan_ref[...].astype(F32), 0.0), axis=1, keepdims=True)
    p_lane = iota((tokens, grid_pairs), 1)
    t_sub = iota((tokens, grid_pairs), 0)
    first = lax.div(p_lane, tokens)
    second = lax.rem(p_lane, tokens)
    seq_first = jnp.sum(jnp.where(first == t_sub, seq, 0.0), axis=0, keepdims=True)
    seq_second = jnp.sum(jnp.where(second == t_sub, seq, 0.0), axis=0, keepdims=True)
    valid = (seq_first == seq_second) & (first[0:1] <= second[0:1])
    before = (iota((grid_pairs, grid_pairs), 0) < iota((grid_pairs, grid_pairs), 1)).astype(BF16)
    rank = dot(jnp.broadcast_to(valid.astype(F32), (8, grid_pairs)).astype(BF16), before)[0:1]
    place = jnp.where(valid, rank, -1.0)
    pick = (iota((PAIR_ROWS, grid_pairs), 0).astype(F32) == place).astype(BF16)
    p_sub = iota((grid_pairs, tokens), 0)
    t_lane = iota((grid_pairs, tokens), 1)
    is_first = lax.div(p_sub, tokens) == t_lane
    is_second = lax.rem(p_sub, tokens) == t_lane
    factor = jnp.where(lax.div(p_sub, tokens) == lax.rem(p_sub, tokens), 1.0, 2.0)
    s1 = dot(pick, jnp.where(is_first, 1.0, 0.0).astype(BF16)).astype(BF16)
    s1_scaled = dot(pick, jnp.where(is_first, factor, 0.0).astype(BF16)).astype(BF16)
    s2 = dot(pick, jnp.where(is_second, 1.0, 0.0).astype(BF16)).astype(BF16)
    token = iota((tokens, tokens), 0)
    slot = iota((tokens, tokens), 1)
    source = ((me + 8 - 2 * (slot >> 2)) & 7) ^ ((slot >> 1) & 1)
    perm = (token == 2 * source + (slot & 1)).astype(BF16)
    s1a_ref[...] = s1
    s2a_ref[...] = s2
    s1g_ref[...] = dot(s1_scaled, perm).astype(BF16)
    s2g_ref[...] = dot(s2, perm).astype(BF16)
    perm_ref[...] = perm


def make_pairs(me, doc_lengths, doc_plan, tokens):
    vmem = pl.BlockSpec(memory_space=pltpu.VMEM)
    sel = jax.ShapeDtypeStruct((PAIR_ROWS, tokens), BF16)
    return pl.pallas_call(
        pairs_kernel,
        out_shape=(sel, sel, sel, sel, jax.ShapeDtypeStruct((tokens, tokens), BF16)),
        in_specs=[pl.BlockSpec(memory_space=pltpu.SMEM), vmem, vmem],
        out_specs=(vmem,) * 5,
        cost_estimate=pl.CostEstimate(flops=2_000_000, bytes_accessed=40_000, transcendentals=0),
        name="pairs",
    )(me, doc_lengths[None, :], doc_plan[None, :])


def assemble_kernel(width, p0, p1, p2, p3, acts_ref, grads_ref):
    rows = []
    for piece in (p0, p1, p2, p3):
        for side in range(2):
            rows.append(piece[side].astype(F32))
    whole = jnp.concatenate(rows, axis=0).astype(BF16)
    acts_ref[...] = whole[:, :width]
    grads_ref[...] = whole[:, width:]


def assemble(pieces, width):
    tokens = sum(p.shape[0] * p.shape[1] for p in pieces)
    total = pieces[0].shape[2]
    vmem = pl.BlockSpec(memory_space=pltpu.VMEM)
    return pl.pallas_call(
        functools.partial(assemble_kernel, width),
        out_shape=(
            jax.ShapeDtypeStruct((tokens, width), BF16),
            jax.ShapeDtypeStruct((tokens, total - width), BF16),
        ),
        in_specs=[vmem] * 4,
        out_specs=(vmem, vmem),
        cost_estimate=pl.CostEstimate(flops=1_000_000, bytes_accessed=600_000, transcendentals=0),
        name="assemble",
    )(*pieces)


def rotate_first_kernel(half_ref, w_ref, x_ref, o_ref):
    o_ref[...] = dot(w_ref[0], x_ref[...], NT)


def rotate_second_kernel(half_ref, w_ref, x_ref, part_ref, perm_ref, o_ref):
    total = (dot(w_ref[0], x_ref[...], NT) + part_ref[...]).astype(BF16)
    mine = dot(perm_ref[...], total, NT).astype(BF16)
    for row in range(o_ref.shape[0]):
        o_ref[row] = mine


def rotate_acts(eigen_a, half, x, part=None, perm=None, copies=0, block=128):
    _, features, _ = eigen_a.shape
    tokens, depth = x.shape
    w_spec = pl.BlockSpec((1, block, depth), lambda i, h: (0, i, h[0]))
    x_spec = pl.BlockSpec((tokens, depth), lambda i, h: (0, 0))
    part_spec = pl.BlockSpec((block, tokens), lambda i, h: (i, 0))
    cost = pl.CostEstimate(
        flops=2 * features * depth * 256, bytes_accessed=features * depth * 2, transcendentals=0
    )
    params = pltpu.CompilerParams(vmem_limit_bytes=24 * 1024 * 1024)
    if part is None:
        return pl.pallas_call(
            rotate_first_kernel,
            out_shape=jax.ShapeDtypeStruct((features, tokens), F32),
            grid_spec=pltpu.PrefetchScalarGridSpec(
                num_scalar_prefetch=1,
                grid=(features // block,),
                in_specs=[w_spec, x_spec],
                out_specs=part_spec,
            ),
            compiler_params=params,
            cost_estimate=cost,
            name="rotate_first",
        )(half, eigen_a, x)
    return pl.pallas_call(
        rotate_second_kernel,
        out_shape=jax.ShapeDtypeStruct((copies, tokens, features), BF16),
        grid_spec=pltpu.PrefetchScalarGridSpec(
            num_scalar_prefetch=1,
            grid=(features // block,),
            in_specs=[w_spec, x_spec, part_spec, pl.BlockSpec((tokens, tokens), lambda i, h: (0, 0))],
            out_specs=pl.BlockSpec((copies, tokens, block), lambda i, h: (0, 0, i)),
        ),
        compiler_params=params,
        cost_estimate=cost,
        name="rotate_second",
    )(half, eigen_a, x, part, perm)


def rotate_grads_kernel(w_ref, x_ref, o_ref):
    o_ref[...] = dot(w_ref[...], x_ref[...], NT).T


def rotate_grads(eigen_s, x, block=128):
    features, depth = eigen_s.shape
    tokens = x.shape[0]
    return pl.pallas_call(
        rotate_grads_kernel,
        out_shape=jax.ShapeDtypeStruct((tokens, features), F32),
        grid=(features // block,),
        in_specs=[
            pl.BlockSpec((block, depth), lambda i: (i, 0)),
            pl.BlockSpec((tokens, depth), lambda i: (0, 0)),
        ],
        out_specs=pl.BlockSpec((tokens, block), lambda i: (0, i)),
        compiler_params=pltpu.CompilerParams(vmem_limit_bytes=24 * 1024 * 1024),
        cost_estimate=pl.CostEstimate(
            flops=2 * features * depth * 256, bytes_accessed=features * depth * 2, transcendentals=0
        ),
        name="rotate_grads",
    )(eigen_s, x)


def split(x):
    high = x.astype(BF16)
    low = (x - high.astype(F32)).astype(BF16)
    return high, low


def correct_kernel(tokens, own_ref, other_ref, a_ref, s1a_ref, s2a_ref, s1g_ref, s2g_ref, o_ref, g_pairs):
    @pl.when(pl.program_id(0) == 0)
    def _():
        g_rot = (own_ref[...] + other_ref[...]).astype(BF16)
        product = dot(s1g_ref[...], g_rot) * dot(s2g_ref[...], g_rot) * (1.0 / tokens)
        high, low = split(product)
        g_pairs[...] = jnp.concatenate([high, high, low], axis=0).T

    a_rot = a_ref[0]
    high, low = split(dot(s1a_ref[...], a_rot) * dot(s2a_ref[...], a_rot))
    a_pairs = jnp.concatenate([high, low, high], axis=0)
    o_ref[...] = dot(g_pairs[...], a_pairs)


def correct(own, other, a_all, s1a, s2a, s1g, s2g):
    tokens, rows = own.shape
    n_row, _, width = a_all.shape
    block = 256
    per = width // block
    g_spec = pl.BlockSpec((tokens, rows), lambda i: (0, 0))
    s_spec = pl.BlockSpec((PAIR_ROWS, tokens), lambda i: (0, 0))
    return pl.pallas_call(
        functools.partial(correct_kernel, tokens),
        out_shape=jax.ShapeDtypeStruct((rows, n_row * width), F32),
        grid=(n_row * per,),
        in_specs=[
            g_spec,
            g_spec,
            pl.BlockSpec((1, tokens, block), lambda i: (i // per, 0, i % per)),
            s_spec,
            s_spec,
            s_spec,
            s_spec,
        ],
        out_specs=pl.BlockSpec((rows, block), lambda i: (0, i)),
        scratch_shapes=[pltpu.VMEM((rows, 3 * PAIR_ROWS), BF16)],
        compiler_params=pltpu.CompilerParams(vmem_limit_bytes=VMEM_LIMIT),
        cost_estimate=pl.CostEstimate(
            flops=2 * rows * n_row * width * 256, bytes_accessed=rows * n_row * width * 4, transcendentals=0
        ),
        name="correct",
    )(own, other, a_all, s1a, s2a, s1g, s2g)


def few_tokens_body(acts, grads, eigen_a, eigen_s_rows, doc_lengths, doc_plan):
    n_row = 8
    tokens = n_row * acts.shape[0]
    me = lax.axis_index("row").astype(I32)[None]
    col = lax.axis_index("col").astype(I32)[None]
    width = acts.shape[1]

    payload = jnp.concatenate([acts, grads], axis=1)
    beside = lax.ppermute(payload, "row", [(i, i ^ 1) for i in range(n_row)])
    both = jnp.stack([payload, beside])
    pieces = [both] + [
        lax.ppermute(both, "row", [(i, (i + 2 * k) % n_row) for i in range(n_row)]) for k in range(1, 4)
    ]
    s1a, s2a, s1g, s2g, perm = make_pairs(me, doc_lengths, doc_plan, tokens)
    acts_own, grads_own = assemble(pieces, width)
    acts_other = lax.ppermute(acts_own, "col", [(0, 1), (1, 0)])
    part = rotate_acts(eigen_a, col, acts_own)
    copies = rotate_acts(eigen_a, 1 - col, acts_other, part, perm, n_row)
    a_all = lax.all_to_all(copies, "row", 0, 0)
    g_own = rotate_grads(eigen_s_rows, grads_own)
    g_other = lax.ppermute(g_own, "col", [(0, 1), (1, 0)])
    return correct(g_own, g_other, a_all, s1a, s2a, s1g, s2g)


def solution(mesh):
    def body(acts, *rest):
        n_row = mesh.shape["row"]
        tokens = n_row * acts.shape[0]
        most = tokens - (N_SEQ - 1)
        pairs = most * (most + 1) // 2 + N_SEQ - 1
        few = n_row == 8 and acts.shape[0] == 2 and mesh.shape["col"] == 2 and pairs <= PAIR_ROWS
        return (few_tokens_body if few else general_body)(acts, *rest)

    return jax.shard_map(
        body,
        mesh=mesh,
        in_specs=(
            P(("grp", "row"), "col"),
            P(("grp", "row"), "col"),
            P("col", "row", None),
            P("row", "col"),
            P("grp"),
            P("grp"),
        ),
        out_specs=P(("grp", "row"), "col"),
        check_vma=False,
    )
```

```python
import functools
import jax
import jax.numpy as jnp
from jax import lax
from jax.experimental import pallas as pl
from jax.experimental.pallas import tpu as pltpu
from jax.sharding import PartitionSpec as P

N_SEQ = 6
PAIR_ROWS = 80
BF16 = jnp.bfloat16
F32 = jnp.float32
I32 = jnp.int32
NT = (((1,), (1,)), ((), ()))
MIB = 1024 * 1024
HBM = pl.BlockSpec(memory_space=pltpu.HBM)
SMEM = pl.BlockSpec(memory_space=pltpu.SMEM)
VMEM = pl.BlockSpec(memory_space=pltpu.VMEM)


def iota(shape, dim):
    return lax.broadcasted_iota(I32, shape, dim)


def dot(a, b, dims=(((1,), (0,)), ((), ()))):
    return lax.dot_general(a, b, dims, preferred_element_type=F32)


def sequence_index(doc_lengths, doc_plan, total_tokens):
    positions = jnp.arange(total_tokens, dtype=I32)
    doc_ends = jnp.cumsum(doc_lengths)
    doc_index = jnp.sum((positions[:, None] >= doc_ends[None, :]).astype(I32), axis=1)
    doc_onehot = (doc_index[:, None] == jnp.arange(doc_lengths.shape[0], dtype=I32)[None, :]).astype(I32)
    return jnp.sum(doc_onehot * doc_plan[None, :], axis=1)


def general_body(acts, grads, eigen_a, eigen_s_rows, doc_lengths, doc_plan):
    act_rows = lax.all_gather(acts, "row", axis=0, tiled=True)
    act_full = lax.all_gather(act_rows, "col", axis=1, tiled=True)
    a_block = dot(eigen_a[0], act_full, NT).astype(BF16)
    a_rot = lax.all_gather(a_block, "row", axis=0, tiled=True)
    grad_terms = dot(eigen_s_rows, lax.all_gather(grads, "row", axis=0, tiled=True), NT)
    g_rot = lax.psum(grad_terms, "col").astype(BF16)
    total_tokens = g_rot.shape[1]
    seq_index = sequence_index(doc_lengths, doc_plan, total_tokens)
    correction = jnp.zeros((g_rot.shape[0], a_rot.shape[0]), F32)
    for sequence in range(N_SEQ):
        inside = (seq_index == sequence).astype(BF16)
        term = dot(g_rot * inside[None, :], a_rot, NT)
        correction = correction + term * term
    return correction / total_tokens


def pairs_kernel(ids_ref, len_ref, plan_ref, s1a_ref, s2a_ref, s1g_ref, s2g_ref, perm_ref):
    docs = len_ref.shape[1]
    tokens = perm_ref.shape[0]
    grid_pairs = tokens * tokens
    me = ids_ref[0]
    upper = (iota((docs, docs), 0) <= iota((docs, docs), 1)).astype(F32)
    ends = dot(jnp.broadcast_to(len_ref[...].astype(F32), (8, docs)), upper)[0:1]
    position = iota((tokens, docs), 0).astype(F32)
    doc = jnp.sum((ends <= position).astype(F32), axis=1, keepdims=True)
    onehot = doc == iota((tokens, docs), 1).astype(F32)
    seq = jnp.sum(jnp.where(onehot, plan_ref[...].astype(F32), 0.0), axis=1, keepdims=True)
    p_lane = iota((tokens, grid_pairs), 1)
    t_sub = iota((tokens, grid_pairs), 0)
    first = lax.div(p_lane, tokens)
    second = lax.rem(p_lane, tokens)
    seq_first = jnp.sum(jnp.where(first == t_sub, seq, 0.0), axis=0, keepdims=True)
    seq_second = jnp.sum(jnp.where(second == t_sub, seq, 0.0), axis=0, keepdims=True)
    valid = (seq_first == seq_second) & (first[0:1] <= second[0:1])
    before = (iota((grid_pairs, grid_pairs), 0) < iota((grid_pairs, grid_pairs), 1)).astype(BF16)
    rank = dot(jnp.broadcast_to(valid.astype(F32), (8, grid_pairs)).astype(BF16), before)[0:1]
    place = jnp.where(valid, rank, -1.0)
    pick = (iota((PAIR_ROWS, grid_pairs), 0).astype(F32) == place).astype(BF16)
    p_sub = iota((grid_pairs, tokens), 0)
    t_lane = iota((grid_pairs, tokens), 1)
    is_first = lax.div(p_sub, tokens) == t_lane
    is_second = lax.rem(p_sub, tokens) == t_lane
    factor = jnp.where(lax.div(p_sub, tokens) == lax.rem(p_sub, tokens), 1.0, 2.0)
    s1 = dot(pick, jnp.where(is_first, 1.0, 0.0).astype(BF16)).astype(BF16)
    s1_scaled = dot(pick, jnp.where(is_first, factor, 0.0).astype(BF16)).astype(BF16)
    s2 = dot(pick, jnp.where(is_second, 1.0, 0.0).astype(BF16)).astype(BF16)
    token = iota((tokens, tokens), 0)
    slot = iota((tokens, tokens), 1)
    source = ((me + 8 - 2 * (slot >> 2)) & 7) ^ ((slot >> 1) & 1)
    perm = (token == 2 * source + (slot & 1)).astype(BF16)
    s1a_ref[...] = s1
    s2a_ref[...] = s2
    s1g_ref[...] = dot(s1_scaled, perm).astype(BF16)
    s2g_ref[...] = dot(s2, perm).astype(BF16)
    perm_ref[...] = perm


def make_pairs(ids, doc_lengths, doc_plan, tokens):
    sel = jax.ShapeDtypeStruct((PAIR_ROWS, tokens), BF16)
    return pl.pallas_call(
        pairs_kernel,
        out_shape=(sel, sel, sel, sel, jax.ShapeDtypeStruct((tokens, tokens), BF16)),
        in_specs=[SMEM, VMEM, VMEM],
        out_specs=(VMEM,) * 5,
        compiler_params=pltpu.CompilerParams(vmem_limit_bytes=2 * MIB),
        cost_estimate=pl.CostEstimate(flops=2_000_000, bytes_accessed=40_000, transcendentals=0),
        name="pairs",
    )(ids, doc_lengths[None, :], doc_plan[None, :])


def pack_kernel(ids_ref, acts_ref, grads_ref, acts_beside_ref, grads_beside_ref, o_ref):
    width = acts_ref.shape[1]
    o_ref[0, :, :width] = acts_ref[...]
    o_ref[0, :, width:] = grads_ref[...]
    o_ref[1, :, :width] = acts_beside_ref[...]
    o_ref[1, :, width:] = grads_beside_ref[...]


def pack(ids, acts, grads, acts_beside, grads_beside):
    rows, width = acts.shape
    return pl.pallas_call(
        pack_kernel,
        out_shape=jax.ShapeDtypeStruct((2, rows, width + grads.shape[1]), BF16),
        in_specs=[SMEM] + [VMEM] * 4,
        out_specs=VMEM,
        compiler_params=pltpu.CompilerParams(vmem_limit_bytes=2 * MIB),
        cost_estimate=pl.CostEstimate(flops=10_000, bytes_accessed=200_000, transcendentals=0),
        name="pack",
    )(ids, acts, grads, acts_beside, grads_beside)


def assemble_kernel(width, p0, p1, p2, p3, basis_ref, perm_ref, acts_ref, grads_ref):
    rows = []
    for piece in (p0, p1, p2, p3):
        for side in range(2):
            rows.append(piece[side].astype(F32))
    whole = jnp.concatenate(rows, axis=0).astype(BF16)
    acts_ref[...] = whole[:, :width]
    grads_ref[...] = whole[:, width:]


def assemble(pieces, basis, perm, width):
    tokens = sum(p.shape[0] * p.shape[1] for p in pieces)
    total = pieces[0].shape[2]
    return pl.pallas_call(
        functools.partial(assemble_kernel, width),
        out_shape=(
            jax.ShapeDtypeStruct((tokens, width), BF16),
            jax.ShapeDtypeStruct((tokens, total - width), BF16),
        ),
        in_specs=[VMEM] * 6,
        out_specs=(VMEM, VMEM),
        compiler_params=pltpu.CompilerParams(vmem_limit_bytes=4 * MIB),
        cost_estimate=pl.CostEstimate(flops=1_000_000, bytes_accessed=600_000, transcendentals=0),
        name="assemble",
    )(*pieces, basis, perm)


def load_kernel(w_ref, o_ref, sem):
    copy = pltpu.make_async_copy(w_ref, o_ref, sem)
    copy.start()
    copy.wait()


def load(w):
    return pl.pallas_call(
        load_kernel,
        out_shape=jax.ShapeDtypeStruct(w.shape, w.dtype),
        in_specs=[HBM],
        out_specs=VMEM,
        scratch_shapes=[pltpu.SemaphoreType.DMA],
        compiler_params=pltpu.CompilerParams(vmem_limit_bytes=42 * MIB),
        cost_estimate=pl.CostEstimate(flops=0, bytes_accessed=w.size * 2, transcendentals=0),
        name="load",
    )(w)


def half_dot(half, w_ref, x_ref):
    depth = x_ref.shape[1]
    columns = pl.ds(pl.multiple_of(half * depth, depth), depth)
    return dot(w_ref[0, :, columns], x_ref[...], NT)


def rotate_first_kernel(ids_ref, w_ref, x_ref, o_ref):
    o_ref[...] = half_dot(ids_ref[1], w_ref, x_ref)


def rotate_second_kernel(ids_ref, w_ref, x_ref, part_ref, perm_ref, o_ref):
    total = (half_dot(1 - ids_ref[1], w_ref, x_ref) + part_ref[...]).astype(BF16)
    mine = dot(perm_ref[...], total, NT).astype(BF16)
    for row in range(o_ref.shape[0]):
        o_ref[row] = mine


def rotate_acts(eigen_a, ids, x, part=None, perm=None, copies=0):
    _, features, _ = eigen_a.shape
    tokens, depth = x.shape
    cost = pl.CostEstimate(
        flops=2 * features * depth * 256, bytes_accessed=features * depth * 2, transcendentals=0
    )
    params = pltpu.CompilerParams(vmem_limit_bytes=4 * MIB)
    if part is None:
        return pl.pallas_call(
            rotate_first_kernel,
            out_shape=jax.ShapeDtypeStruct((features, tokens), F32),
            in_specs=[SMEM, VMEM, VMEM],
            out_specs=VMEM,
            compiler_params=params,
            cost_estimate=cost,
            name="rotate_first",
        )(ids, eigen_a, x)
    return pl.pallas_call(
        rotate_second_kernel,
        out_shape=jax.ShapeDtypeStruct((copies, tokens, features), BF16),
        in_specs=[SMEM, VMEM, VMEM, VMEM, VMEM],
        out_specs=VMEM,
        compiler_params=params,
        cost_estimate=cost,
        name="rotate_second",
    )(ids, eigen_a, x, part, perm)


def rotate_grads_kernel(w_ref, x_ref, o_ref, held, sems):
    parts = sems.shape[0]
    block = w_ref.shape[0] // parts
    copies = []
    for part in range(parts):
        rows = slice(part * block, (part + 1) * block)
        copies.append(pltpu.make_async_copy(w_ref.at[rows, :], held.at[rows, :], sems.at[part]))
        copies[-1].start()
    for part in range(parts):
        rows = slice(part * block, (part + 1) * block)
        copies[part].wait()
        o_ref[:, rows] = dot(held[rows, :], x_ref[...], NT).T


def rotate_grads(eigen_s, x):
    features, depth = eigen_s.shape
    tokens = x.shape[0]
    parts = features // 256
    return pl.pallas_call(
        rotate_grads_kernel,
        out_shape=jax.ShapeDtypeStruct((tokens, features), F32),
        in_specs=[HBM, VMEM],
        out_specs=VMEM,
        scratch_shapes=[pltpu.VMEM((features, depth), BF16), pltpu.SemaphoreType.DMA((parts,))],
        compiler_params=pltpu.CompilerParams(vmem_limit_bytes=52 * MIB),
        cost_estimate=pl.CostEstimate(
            flops=2 * features * depth * 256, bytes_accessed=features * depth * 2, transcendentals=0
        ),
        name="rotate_grads",
    )(eigen_s, x)


def split(x):
    high = x.astype(BF16)
    low = (x - high.astype(F32)).astype(BF16)
    return high, low


def correct_kernel(own_ref, other_ref, a_ref, s1a_ref, s2a_ref, s1g_ref, s2g_ref, o_ref, buffer, g_pairs, sems):
    tokens = own_ref.shape[0]
    n_block, _, width = a_ref.shape
    g_rot = (own_ref[...] + other_ref[...]).astype(BF16)
    product = dot(s1g_ref[...], g_rot) * dot(s2g_ref[...], g_rot) * (1.0 / tokens)
    high, low = split(product)
    g_pairs[...] = jnp.concatenate([high, high, low], axis=0).T
    copies = []
    for block in range(n_block):
        a_rot = a_ref[block]
        high, low = split(dot(s1a_ref[...], a_rot) * dot(s2a_ref[...], a_rot))
        columns = slice(block * width, (block + 1) * width)
        buffer[:, columns] = dot(g_pairs[...], jnp.concatenate([high, low, high], axis=0))
        copies.append(pltpu.make_async_copy(buffer.at[:, columns], o_ref.at[:, columns], sems.at[block]))
        copies[-1].start()
    for copy in copies:
        copy.wait()


def correct(own, other, a_all, s1a, s2a, s1g, s2g):
    tokens, rows = own.shape
    n_row, _, width = a_all.shape
    return pl.pallas_call(
        correct_kernel,
        out_shape=jax.ShapeDtypeStruct((rows, n_row * width), F32),
        in_specs=[VMEM] * 7,
        out_specs=pl.BlockSpec(memory_space=pl.ANY),
        scratch_shapes=[
            pltpu.VMEM((rows, n_row * width), F32),
            pltpu.VMEM((rows, 3 * PAIR_ROWS), BF16),
            pltpu.SemaphoreType.DMA((n_row,)),
        ],
        compiler_params=pltpu.CompilerParams(vmem_limit_bytes=32 * MIB),
        cost_estimate=pl.CostEstimate(
            flops=2 * rows * n_row * width * 256, bytes_accessed=rows * n_row * width * 4, transcendentals=0
        ),
        name="correct",
    )(own, other, a_all, s1a, s2a, s1g, s2g)


def few_tokens_body(acts, grads, eigen_a, eigen_s_rows, doc_lengths, doc_plan):
    n_row = 8
    tokens = n_row * acts.shape[0]
    ids = jnp.stack([lax.axis_index("row"), lax.axis_index("col")]).astype(I32)
    width = acts.shape[1]

    across = [(i, i ^ 1) for i in range(n_row)]
    acts_beside = lax.ppermute(acts, "row", across)
    grads_beside = lax.ppermute(grads, "row", across)
    both = pack(ids, acts, grads, acts_beside, grads_beside)
    pieces = [both] + [
        lax.ppermute(both, "row", [(i, (i + 2 * k) % n_row) for i in range(n_row)]) for k in range(1, 4)
    ]
    s1a, s2a, s1g, s2g, perm = make_pairs(ids, doc_lengths, doc_plan, tokens)
    basis = load(eigen_a)
    acts_own, grads_own = assemble(pieces, basis, perm, width)
    acts_other = lax.ppermute(acts_own, "col", [(0, 1), (1, 0)])
    part = rotate_acts(basis, ids, acts_own)
    copies = rotate_acts(basis, ids, acts_other, part, perm, n_row)
    a_all = lax.all_to_all(copies, "row", 0, 0)
    g_own = rotate_grads(eigen_s_rows, grads_own)
    g_other = lax.ppermute(g_own, "col", [(0, 1), (1, 0)])
    return correct(g_own, g_other, a_all, s1a, s2a, s1g, s2g)


def solution(mesh):
    def body(acts, *rest):
        n_row = mesh.shape["row"]
        tokens = n_row * acts.shape[0]
        most = tokens - (N_SEQ - 1)
        pairs = most * (most + 1) // 2 + N_SEQ - 1
        few = n_row == 8 and acts.shape[0] == 2 and mesh.shape["col"] == 2 and pairs <= PAIR_ROWS
        return (few_tokens_body if few else general_body)(acts, *rest)

    return jax.shard_map(
        body,
        mesh=mesh,
        in_specs=(
            P(("grp", "row"), "col"),
            P(("grp", "row"), "col"),
            P("col", "row", None),
            P("row", "col"),
            P("grp"),
            P("grp"),
        ),
        out_specs=P(("grp", "row"), "col"),
        check_vma=False,
    )
```

```python
import functools
import jax
import jax.numpy as jnp
from jax import lax
from jax.experimental import pallas as pl
from jax.experimental.pallas import tpu as pltpu
from jax.sharding import PartitionSpec as P

N_SEQ = 6
PAIR_ROWS = 80
BF16 = jnp.bfloat16
F32 = jnp.float32
I32 = jnp.int32
NT = (((1,), (1,)), ((), ()))
MIB = 1024 * 1024
HBM = pl.BlockSpec(memory_space=pltpu.HBM)
VMEM = pl.BlockSpec(memory_space=pltpu.VMEM)


def iota(shape, dim):
    return lax.broadcasted_iota(I32, shape, dim)


def dot(a, b, dims=(((1,), (0,)), ((), ()))):
    return lax.dot_general(a, b, dims, preferred_element_type=F32)


def sequence_index(doc_lengths, doc_plan, total_tokens):
    positions = jnp.arange(total_tokens, dtype=I32)
    doc_ends = jnp.cumsum(doc_lengths)
    doc_index = jnp.sum((positions[:, None] >= doc_ends[None, :]).astype(I32), axis=1)
    doc_onehot = (doc_index[:, None] == jnp.arange(doc_lengths.shape[0], dtype=I32)[None, :]).astype(I32)
    return jnp.sum(doc_onehot * doc_plan[None, :], axis=1)


def general_body(acts, grads, eigen_a, eigen_s_rows, doc_lengths, doc_plan):
    act_rows = lax.all_gather(acts, "row", axis=0, tiled=True)
    act_full = lax.all_gather(act_rows, "col", axis=1, tiled=True)
    a_block = dot(eigen_a[0], act_full, NT).astype(BF16)
    a_rot = lax.all_gather(a_block, "row", axis=0, tiled=True)
    grad_terms = dot(eigen_s_rows, lax.all_gather(grads, "row", axis=0, tiled=True), NT)
    g_rot = lax.psum(grad_terms, "col").astype(BF16)
    total_tokens = g_rot.shape[1]
    seq_index = sequence_index(doc_lengths, doc_plan, total_tokens)
    correction = jnp.zeros((g_rot.shape[0], a_rot.shape[0]), F32)
    for sequence in range(N_SEQ):
        inside = (seq_index == sequence).astype(BF16)
        term = dot(g_rot * inside[None, :], a_rot, NT)
        correction = correction + term * term
    return correction / total_tokens


def pairs_kernel(len_ref, plan_ref, s1a_ref, s2a_ref, s1g_ref, s2g_ref, perm_ref):
    docs = len_ref.shape[1]
    tokens = perm_ref.shape[0]
    grid_pairs = tokens * tokens
    me = lax.axis_index("row")
    upper = (iota((docs, docs), 0) <= iota((docs, docs), 1)).astype(F32)
    ends = dot(jnp.broadcast_to(len_ref[...].astype(F32), (8, docs)), upper)[0:1]
    position = iota((tokens, docs), 0).astype(F32)
    doc = jnp.sum((ends <= position).astype(F32), axis=1, keepdims=True)
    onehot = doc == iota((tokens, docs), 1).astype(F32)
    seq = jnp.sum(jnp.where(onehot, plan_ref[...].astype(F32), 0.0), axis=1, keepdims=True)
    p_lane = iota((tokens, grid_pairs), 1)
    t_sub = iota((tokens, grid_pairs), 0)
    first = lax.div(p_lane, tokens)
    second = lax.rem(p_lane, tokens)
    seq_first = jnp.sum(jnp.where(first == t_sub, seq, 0.0), axis=0, keepdims=True)
    seq_second = jnp.sum(jnp.where(second == t_sub, seq, 0.0), axis=0, keepdims=True)
    valid = (seq_first == seq_second) & (first[0:1] <= second[0:1])
    before = (iota((grid_pairs, grid_pairs), 0) < iota((grid_pairs, grid_pairs), 1)).astype(BF16)
    rank = dot(jnp.broadcast_to(valid.astype(F32), (8, grid_pairs)).astype(BF16), before)[0:1]
    place = jnp.where(valid, rank, -1.0)
    pick = (iota((PAIR_ROWS, grid_pairs), 0).astype(F32) == place).astype(BF16)
    p_sub = iota((grid_pairs, tokens), 0)
    t_lane = iota((grid_pairs, tokens), 1)
    is_first = lax.div(p_sub, tokens) == t_lane
    is_second = lax.rem(p_sub, tokens) == t_lane
    factor = jnp.where(lax.div(p_sub, tokens) == lax.rem(p_sub, tokens), 1.0, 2.0)
    s1 = dot(pick, jnp.where(is_first, 1.0, 0.0).astype(BF16)).astype(BF16)
    s1_scaled = dot(pick, jnp.where(is_first, factor, 0.0).astype(BF16)).astype(BF16)
    s2 = dot(pick, jnp.where(is_second, 1.0, 0.0).astype(BF16)).astype(BF16)
    token = iota((tokens, tokens), 0)
    slot = iota((tokens, tokens), 1)
    source = ((me + 8 - 2 * (slot >> 2)) & 7) ^ ((slot >> 1) & 1)
    perm = (token == 2 * source + (slot & 1)).astype(BF16)
    s1a_ref[...] = s1
    s2a_ref[...] = s2
    s1g_ref[...] = dot(s1_scaled, perm).astype(BF16)
    s2g_ref[...] = dot(s2, perm).astype(BF16)
    perm_ref[...] = perm


def make_pairs(doc_lengths, doc_plan, tokens):
    sel = jax.ShapeDtypeStruct((PAIR_ROWS, tokens), BF16)
    return pl.pallas_call(
        pairs_kernel,
        out_shape=(sel, sel, sel, sel, jax.ShapeDtypeStruct((tokens, tokens), BF16)),
        in_specs=[VMEM, VMEM],
        out_specs=(VMEM,) * 5,
        compiler_params=pltpu.CompilerParams(vmem_limit_bytes=2 * MIB),
        cost_estimate=pl.CostEstimate(flops=2_000_000, bytes_accessed=40_000, transcendentals=0),
        name="pairs",
    )(doc_lengths[None, :], doc_plan[None, :])


def pack_kernel(acts_ref, grads_ref, o_ref, sems):
    width = acts_ref.shape[1]
    copies = (
        pltpu.make_async_copy(acts_ref, o_ref.at[:, :width], sems.at[0]),
        pltpu.make_async_copy(grads_ref, o_ref.at[:, width:], sems.at[1]),
    )
    for copy in copies:
        copy.start()
    for copy in copies:
        copy.wait()


def pack(acts, grads):
    rows, width = acts.shape
    return pl.pallas_call(
        pack_kernel,
        out_shape=jax.ShapeDtypeStruct((rows, width + grads.shape[1]), BF16),
        in_specs=[HBM, HBM],
        out_specs=VMEM,
        scratch_shapes=[pltpu.SemaphoreType.DMA((2,))],
        cost_estimate=pl.CostEstimate(flops=0, bytes_accessed=80_000, transcendentals=0),
        name="pack",
    )(acts, grads)


def stage_kernel(own_ref, o_ref):
    o_ref[...] = own_ref[...]


def stage(own):
    return pl.pallas_call(
        stage_kernel,
        out_shape=jax.ShapeDtypeStruct(own.shape, BF16),
        in_specs=[VMEM],
        out_specs=VMEM,
        compiler_params=pltpu.CompilerParams(vmem_limit_bytes=2 * MIB),
        cost_estimate=pl.CostEstimate(flops=10_000, bytes_accessed=2_000_000, transcendentals=0),
        name="stage",
    )(own)


def merge_kernel(own_ref, beside_ref, o_ref):
    o_ref[0] = own_ref[...]
    o_ref[1] = beside_ref[...]


def merge(own, beside):
    return pl.pallas_call(
        merge_kernel,
        out_shape=jax.ShapeDtypeStruct((2,) + own.shape, BF16),
        in_specs=[VMEM] * 2,
        out_specs=VMEM,
        compiler_params=pltpu.CompilerParams(vmem_limit_bytes=2 * MIB),
        cost_estimate=pl.CostEstimate(flops=10_000, bytes_accessed=150_000, transcendentals=0),
        name="merge",
    )(own, beside)


def assemble_kernel(width, p0, p1, p2, p3, basis_ref, perm_ref, acts_ref, grads_ref):
    rows = []
    for piece in (p0, p1, p2, p3):
        for side in range(2):
            rows.append(piece[side].astype(F32))
    whole = jnp.concatenate(rows, axis=0).astype(BF16)
    acts_ref[...] = whole[:, :width]
    grads_ref[...] = whole[:, width:]


def assemble(pieces, basis, perm, width):
    tokens = sum(p.shape[0] * p.shape[1] for p in pieces)
    total = pieces[0].shape[2]
    return pl.pallas_call(
        functools.partial(assemble_kernel, width),
        out_shape=(
            jax.ShapeDtypeStruct((tokens, width), BF16),
            jax.ShapeDtypeStruct((tokens, total - width), BF16),
        ),
        in_specs=[VMEM] * 6,
        out_specs=(VMEM, VMEM),
        compiler_params=pltpu.CompilerParams(vmem_limit_bytes=4 * MIB),
        cost_estimate=pl.CostEstimate(flops=1_000_000, bytes_accessed=600_000, transcendentals=0),
        name="assemble",
    )(*pieces, basis, perm)


def load_kernel(w_ref, o_ref, sem):
    copy = pltpu.make_async_copy(w_ref, o_ref, sem)
    copy.start()
    copy.wait()


def load(w):
    return pl.pallas_call(
        load_kernel,
        out_shape=jax.ShapeDtypeStruct(w.shape, w.dtype),
        in_specs=[HBM],
        out_specs=VMEM,
        scratch_shapes=[pltpu.SemaphoreType.DMA],
        compiler_params=pltpu.CompilerParams(vmem_limit_bytes=42 * MIB),
        cost_estimate=pl.CostEstimate(flops=0, bytes_accessed=w.size * 2, transcendentals=0),
        name="load",
    )(w)


def half_dot(half, w_ref, x_ref):
    depth = x_ref.shape[1]
    columns = pl.ds(pl.multiple_of(half * depth, depth), depth)
    return dot(w_ref[0, :, columns], x_ref[...], NT)


def rotate_first_kernel(w_ref, x_ref, o_ref):
    o_ref[...] = half_dot(lax.axis_index("col"), w_ref, x_ref)


def rotate_second_kernel(w_ref, x_ref, part_ref, perm_ref, o_ref):
    total = (half_dot(1 - lax.axis_index("col"), w_ref, x_ref) + part_ref[...]).astype(BF16)
    mine = dot(perm_ref[...], total, NT).astype(BF16)
    for row in range(o_ref.shape[0]):
        o_ref[row] = mine


def rotate_acts(eigen_a, x, part=None, perm=None, copies=0):
    _, features, _ = eigen_a.shape
    tokens, depth = x.shape
    cost = pl.CostEstimate(
        flops=2 * features * depth * 256, bytes_accessed=features * depth * 2, transcendentals=0
    )
    params = pltpu.CompilerParams(vmem_limit_bytes=4 * MIB)
    if part is None:
        return pl.pallas_call(
            rotate_first_kernel,
            out_shape=jax.ShapeDtypeStruct((features, tokens), F32),
            in_specs=[VMEM, VMEM],
            out_specs=VMEM,
            compiler_params=params,
            cost_estimate=cost,
            name="rotate_first",
        )(eigen_a, x)
    return pl.pallas_call(
        rotate_second_kernel,
        out_shape=jax.ShapeDtypeStruct((copies, tokens, features), BF16),
        in_specs=[VMEM] * 4,
        out_specs=VMEM,
        compiler_params=params,
        cost_estimate=cost,
        name="rotate_second",
    )(eigen_a, x, part, perm)


def rotate_grads_kernel(ahead, w_ref, x_ref, o_ref, held, sems):
    parts = sems.shape[0]
    block = w_ref.shape[0] // parts
    spans = [slice(part * block, (part + 1) * block) for part in range(parts)]
    copies = [
        pltpu.make_async_copy(w_ref.at[rows, :], held.at[rows, :], sems.at[part]) for part, rows in enumerate(spans)
    ]
    for part in range(ahead):
        copies[part].start()
    for part, rows in enumerate(spans):
        copies[part].wait()
        if part + ahead < parts:
            copies[part + ahead].start()
        o_ref[:, rows] = dot(held[rows, :], x_ref[...], NT).T


def rotate_grads(eigen_s, x):
    features, depth = eigen_s.shape
    tokens = x.shape[0]
    parts = features // 128
    return pl.pallas_call(
        functools.partial(rotate_grads_kernel, 3),
        out_shape=jax.ShapeDtypeStruct((tokens, features), F32),
        in_specs=[HBM, VMEM],
        out_specs=VMEM,
        scratch_shapes=[pltpu.VMEM((features, depth), BF16), pltpu.SemaphoreType.DMA((parts,))],
        compiler_params=pltpu.CompilerParams(vmem_limit_bytes=52 * MIB),
        cost_estimate=pl.CostEstimate(
            flops=2 * features * depth * 256, bytes_accessed=features * depth * 2, transcendentals=0
        ),
        name="rotate_grads",
    )(eigen_s, x)


def split(x):
    high = x.astype(BF16)
    low = (x - high.astype(F32)).astype(BF16)
    return high, low


def correct_kernel(own_ref, other_ref, a_ref, s1a_ref, s2a_ref, s1g_ref, s2g_ref, o_ref, buffer, g_pairs, sems):
    tokens = own_ref.shape[0]
    n_block, _, width = a_ref.shape
    g_rot = (own_ref[...] + other_ref[...]).astype(BF16)
    product = dot(s1g_ref[...], g_rot) * dot(s2g_ref[...], g_rot) * (1.0 / tokens)
    high, low = split(product)
    g_pairs[...] = jnp.concatenate([high, high, low], axis=0).T
    copies = []
    for block in range(n_block):
        a_rot = a_ref[block]
        high, low = split(dot(s1a_ref[...], a_rot) * dot(s2a_ref[...], a_rot))
        columns = slice(block * width, (block + 1) * width)
        buffer[:, columns] = dot(g_pairs[...], jnp.concatenate([high, low, high], axis=0))
        copies.append(pltpu.make_async_copy(buffer.at[:, columns], o_ref.at[:, columns], sems.at[block]))
        copies[-1].start()
    for copy in copies:
        copy.wait()


def correct(own, other, a_all, s1a, s2a, s1g, s2g):
    tokens, rows = own.shape
    n_row, _, width = a_all.shape
    return pl.pallas_call(
        correct_kernel,
        out_shape=jax.ShapeDtypeStruct((rows, n_row * width), F32),
        in_specs=[VMEM] * 7,
        out_specs=pl.BlockSpec(memory_space=pl.ANY),
        scratch_shapes=[
            pltpu.VMEM((rows, n_row * width), F32),
            pltpu.VMEM((rows, 3 * PAIR_ROWS), BF16),
            pltpu.SemaphoreType.DMA((n_row,)),
        ],
        compiler_params=pltpu.CompilerParams(vmem_limit_bytes=32 * MIB),
        cost_estimate=pl.CostEstimate(
            flops=2 * rows * n_row * width * 256, bytes_accessed=rows * n_row * width * 4, transcendentals=0
        ),
        name="correct",
    )(own, other, a_all, s1a, s2a, s1g, s2g)


def few_tokens_body(acts, grads, eigen_a, eigen_s_rows, doc_lengths, doc_plan):
    n_row = 8
    tokens = n_row * acts.shape[0]
    width = acts.shape[1]

    own = pack(acts, grads)
    beside = lax.ppermute(own, "row", [(i, i ^ 1) for i in range(n_row)])
    both = merge(stage(own), beside)
    pieces = [both] + [
        lax.ppermute(both, "row", [(i, (i + 2 * k) % n_row) for i in range(n_row)]) for k in range(1, 4)
    ]
    basis = load(eigen_a)
    s1a, s2a, s1g, s2g, perm = make_pairs(doc_lengths, doc_plan, tokens)
    acts_own, grads_own = assemble(pieces, basis, perm, width)
    acts_other = lax.ppermute(acts_own, "col", [(0, 1), (1, 0)])
    part = rotate_acts(basis, acts_own)
    copies = rotate_acts(basis, acts_other, part, perm, n_row)
    a_all = lax.all_to_all(copies, "row", 0, 0)
    g_own = rotate_grads(eigen_s_rows, grads_own)
    g_other = lax.ppermute(g_own, "col", [(0, 1), (1, 0)])
    return correct(g_own, g_other, a_all, s1a, s2a, s1g, s2g)


def solution(mesh):
    def body(acts, *rest):
        n_row = mesh.shape["row"]
        tokens = n_row * acts.shape[0]
        most = tokens - (N_SEQ - 1)
        pairs = most * (most + 1) // 2 + N_SEQ - 1
        few = n_row == 8 and acts.shape[0] == 2 and mesh.shape["col"] == 2 and pairs <= PAIR_ROWS
        return (few_tokens_body if few else general_body)(acts, *rest)

    return jax.shard_map(
        body,
        mesh=mesh,
        in_specs=(
            P(("grp", "row"), "col"),
            P(("grp", "row"), "col"),
            P("col", "row", None),
            P("row", "col"),
            P("grp"),
            P("grp"),
        ),
        out_specs=P(("grp", "row"), "col"),
        check_vma=False,
    )
```

```python
import functools
import jax
import jax.numpy as jnp
from jax import lax
from jax.experimental import pallas as pl
from jax.experimental.pallas import tpu as pltpu
from jax.sharding import PartitionSpec as P

N_SEQ = 6
PAIR_ROWS = 80
BF16 = jnp.bfloat16
F32 = jnp.float32
I32 = jnp.int32
NT = (((1,), (1,)), ((), ()))
MIB = 1024 * 1024
HBM = pl.BlockSpec(memory_space=pltpu.HBM)
VMEM = pl.BlockSpec(memory_space=pltpu.VMEM)


def iota(shape, dim):
    return lax.broadcasted_iota(I32, shape, dim)


def dot(a, b, dims=(((1,), (0,)), ((), ()))):
    return lax.dot_general(a, b, dims, preferred_element_type=F32)


def sequence_index(doc_lengths, doc_plan, total_tokens):
    positions = jnp.arange(total_tokens, dtype=I32)
    doc_ends = jnp.cumsum(doc_lengths)
    doc_index = jnp.sum((positions[:, None] >= doc_ends[None, :]).astype(I32), axis=1)
    doc_onehot = (doc_index[:, None] == jnp.arange(doc_lengths.shape[0], dtype=I32)[None, :]).astype(I32)
    return jnp.sum(doc_onehot * doc_plan[None, :], axis=1)


def general_body(acts, grads, eigen_a, eigen_s_rows, doc_lengths, doc_plan):
    act_rows = lax.all_gather(acts, "row", axis=0, tiled=True)
    act_full = lax.all_gather(act_rows, "col", axis=1, tiled=True)
    a_block = dot(eigen_a[0], act_full, NT).astype(BF16)
    a_rot = lax.all_gather(a_block, "row", axis=0, tiled=True)
    grad_terms = dot(eigen_s_rows, lax.all_gather(grads, "row", axis=0, tiled=True), NT)
    g_rot = lax.psum(grad_terms, "col").astype(BF16)
    total_tokens = g_rot.shape[1]
    seq_index = sequence_index(doc_lengths, doc_plan, total_tokens)
    correction = jnp.zeros((g_rot.shape[0], a_rot.shape[0]), F32)
    for sequence in range(N_SEQ):
        inside = (seq_index == sequence).astype(BF16)
        term = dot(g_rot * inside[None, :], a_rot, NT)
        correction = correction + term * term
    return correction / total_tokens


def pairs_kernel(len_ref, plan_ref, s1a_ref, s2a_ref, s1g_ref, s2g_ref, perm_ref):
    docs = len_ref.shape[1]
    tokens = perm_ref.shape[0]
    grid_pairs = tokens * tokens
    me = lax.axis_index("row")
    upper = (iota((docs, docs), 0) <= iota((docs, docs), 1)).astype(F32)
    ends = dot(jnp.broadcast_to(len_ref[...].astype(F32), (8, docs)), upper)[0:1]
    position = iota((tokens, docs), 0).astype(F32)
    doc = jnp.sum((ends <= position).astype(F32), axis=1, keepdims=True)
    onehot = doc == iota((tokens, docs), 1).astype(F32)
    seq = jnp.sum(jnp.where(onehot, plan_ref[...].astype(F32), 0.0), axis=1, keepdims=True)
    p_lane = iota((tokens, grid_pairs), 1)
    t_sub = iota((tokens, grid_pairs), 0)
    first = lax.div(p_lane, tokens)
    second = lax.rem(p_lane, tokens)
    seq_first = jnp.sum(jnp.where(first == t_sub, seq, 0.0), axis=0, keepdims=True)
    seq_second = jnp.sum(jnp.where(second == t_sub, seq, 0.0), axis=0, keepdims=True)
    valid = (seq_first == seq_second) & (first[0:1] <= second[0:1])
    before = (iota((grid_pairs, grid_pairs), 0) < iota((grid_pairs, grid_pairs), 1)).astype(BF16)
    rank = dot(jnp.broadcast_to(valid.astype(F32), (8, grid_pairs)).astype(BF16), before)[0:1]
    place = jnp.where(valid, rank, -1.0)
    pick = (iota((PAIR_ROWS, grid_pairs), 0).astype(F32) == place).astype(BF16)
    p_sub = iota((grid_pairs, tokens), 0)
    t_lane = iota((grid_pairs, tokens), 1)
    is_first = lax.div(p_sub, tokens) == t_lane
    is_second = lax.rem(p_sub, tokens) == t_lane
    factor = jnp.where(lax.div(p_sub, tokens) == lax.rem(p_sub, tokens), 1.0, 2.0)
    s1 = dot(pick, jnp.where(is_first, 1.0, 0.0).astype(BF16)).astype(BF16)
    s1_scaled = dot(pick, jnp.where(is_first, factor, 0.0).astype(BF16)).astype(BF16)
    s2 = dot(pick, jnp.where(is_second, 1.0, 0.0).astype(BF16)).astype(BF16)
    token = iota((tokens, tokens), 0)
    slot = iota((tokens, tokens), 1)
    source = ((me + 8 - 2 * (slot >> 2)) & 7) ^ ((slot >> 1) & 1)
    perm = (token == 2 * source + (slot & 1)).astype(BF16)
    s1a_ref[...] = s1
    s2a_ref[...] = s2
    s1g_ref[...] = dot(s1_scaled, perm).astype(BF16)
    s2g_ref[...] = dot(s2, perm).astype(BF16)
    perm_ref[...] = perm


def make_pairs(doc_lengths, doc_plan, tokens):
    sel = jax.ShapeDtypeStruct((PAIR_ROWS, tokens), BF16)
    return pl.pallas_call(
        pairs_kernel,
        out_shape=(sel, sel, sel, sel, jax.ShapeDtypeStruct((tokens, tokens), BF16)),
        in_specs=[VMEM, VMEM],
        out_specs=(VMEM,) * 5,
        compiler_params=pltpu.CompilerParams(vmem_limit_bytes=2 * MIB),
        cost_estimate=pl.CostEstimate(flops=2_000_000, bytes_accessed=40_000, transcendentals=0),
        name="pairs",
    )(doc_lengths[None, :], doc_plan[None, :])


def pack_kernel(acts_ref, grads_ref, o_ref, sems):
    width = acts_ref.shape[1]
    copies = (
        pltpu.make_async_copy(acts_ref, o_ref.at[:, :width], sems.at[0]),
        pltpu.make_async_copy(grads_ref, o_ref.at[:, width:], sems.at[1]),
    )
    for copy in copies:
        copy.start()
    for copy in copies:
        copy.wait()


def pack(acts, grads):
    rows, width = acts.shape
    return pl.pallas_call(
        pack_kernel,
        out_shape=jax.ShapeDtypeStruct((rows, width + grads.shape[1]), BF16),
        in_specs=[HBM, HBM],
        out_specs=HBM,
        scratch_shapes=[pltpu.SemaphoreType.DMA((2,))],
        cost_estimate=pl.CostEstimate(flops=0, bytes_accessed=80_000, transcendentals=0),
        name="pack",
    )(acts, grads)


def stage_kernel(own_ref, o_ref):
    o_ref[...] = own_ref[...]


def stage(own):
    return pl.pallas_call(
        stage_kernel,
        out_shape=jax.ShapeDtypeStruct(own.shape, BF16),
        in_specs=[VMEM],
        out_specs=VMEM,
        compiler_params=pltpu.CompilerParams(vmem_limit_bytes=2 * MIB),
        cost_estimate=pl.CostEstimate(flops=10_000, bytes_accessed=2_000_000, transcendentals=0),
        name="stage",
    )(own)


def merge_kernel(own_ref, beside_ref, o_ref):
    o_ref[0] = own_ref[...]
    o_ref[1] = beside_ref[...]


def merge(own, beside):
    return pl.pallas_call(
        merge_kernel,
        out_shape=jax.ShapeDtypeStruct((2,) + own.shape, BF16),
        in_specs=[VMEM] * 2,
        out_specs=VMEM,
        compiler_params=pltpu.CompilerParams(vmem_limit_bytes=2 * MIB),
        cost_estimate=pl.CostEstimate(flops=10_000, bytes_accessed=150_000, transcendentals=0),
        name="merge",
    )(own, beside)


def assemble_kernel(width, p0, p1, p2, p3, basis_ref, perm_ref, acts_ref, grads_ref):
    rows = []
    for piece in (p0, p1, p2, p3):
        for side in range(2):
            rows.append(piece[side].astype(F32))
    whole = jnp.concatenate(rows, axis=0).astype(BF16)
    acts_ref[...] = whole[:, :width]
    grads_ref[...] = whole[:, width:]


def assemble(pieces, basis, perm, width):
    tokens = sum(p.shape[0] * p.shape[1] for p in pieces)
    total = pieces[0].shape[2]
    return pl.pallas_call(
        functools.partial(assemble_kernel, width),
        out_shape=(
            jax.ShapeDtypeStruct((tokens, width), BF16),
            jax.ShapeDtypeStruct((tokens, total - width), BF16),
        ),
        in_specs=[VMEM] * 6,
        out_specs=(VMEM, VMEM),
        compiler_params=pltpu.CompilerParams(vmem_limit_bytes=4 * MIB),
        cost_estimate=pl.CostEstimate(flops=1_000_000, bytes_accessed=600_000, transcendentals=0),
        name="assemble",
    )(*pieces, basis, perm)


def load_kernel(w_ref, o_ref, sem):
    copy = pltpu.make_async_copy(w_ref, o_ref, sem)
    copy.start()
    copy.wait()


def load(w):
    return pl.pallas_call(
        load_kernel,
        out_shape=jax.ShapeDtypeStruct(w.shape, w.dtype),
        in_specs=[HBM],
        out_specs=VMEM,
        scratch_shapes=[pltpu.SemaphoreType.DMA],
        compiler_params=pltpu.CompilerParams(vmem_limit_bytes=42 * MIB),
        cost_estimate=pl.CostEstimate(flops=0, bytes_accessed=w.size * 2, transcendentals=0),
        name="load",
    )(w)


def row_dots(w_ref, x, first, last, columns=slice(None), rows=128):
    return jnp.concatenate([dot(w_ref[i : i + rows, columns], x, NT) for i in range(first, last, rows)], axis=0)


def half_dot(half, w_ref, x_ref):
    depth = x_ref.shape[1]
    columns = pl.ds(pl.multiple_of(half * depth, depth), depth)
    return row_dots(w_ref.at[0], x_ref[...], 0, w_ref.shape[1], columns)


def rotate_first_kernel(w_ref, x_ref, o_ref):
    o_ref[...] = half_dot(lax.axis_index("col"), w_ref, x_ref)


def rotate_second_kernel(w_ref, x_ref, part_ref, perm_ref, o_ref):
    total = (half_dot(1 - lax.axis_index("col"), w_ref, x_ref) + part_ref[...]).astype(BF16)
    mine = dot(perm_ref[...], total, NT).astype(BF16)
    for row in range(o_ref.shape[0]):
        o_ref[row] = mine


def rotate_acts(eigen_a, x, part=None, perm=None, copies=0):
    _, features, _ = eigen_a.shape
    tokens, depth = x.shape
    cost = pl.CostEstimate(
        flops=2 * features * depth * 256, bytes_accessed=features * depth * 2, transcendentals=0
    )
    params = pltpu.CompilerParams(vmem_limit_bytes=4 * MIB)
    if part is None:
        return pl.pallas_call(
            rotate_first_kernel,
            out_shape=jax.ShapeDtypeStruct((features, tokens), F32),
            in_specs=[VMEM, VMEM],
            out_specs=VMEM,
            compiler_params=params,
            cost_estimate=cost,
            name="rotate_first",
        )(eigen_a, x)
    return pl.pallas_call(
        rotate_second_kernel,
        out_shape=jax.ShapeDtypeStruct((copies, tokens, features), BF16),
        in_specs=[VMEM] * 4,
        out_specs=VMEM,
        compiler_params=params,
        cost_estimate=cost,
        name="rotate_second",
    )(eigen_a, x, part, perm)


def rotate_grads_kernel(w_ref, x_ref, o_ref, held, sems):
    parts = sems.shape[0]
    block = w_ref.shape[0] // parts
    spans = [slice(part * block, (part + 1) * block) for part in range(parts)]
    copies = [
        pltpu.make_async_copy(w_ref.at[rows, :], held.at[rows, :], sems.at[part]) for part, rows in enumerate(spans)
    ]
    for copy in copies:
        copy.start()
    for copy, rows in zip(copies, spans):
        copy.wait()
        o_ref[:, rows] = row_dots(held, x_ref[...], rows.start, rows.stop).T


def rotate_grads(eigen_s, x):
    features, depth = eigen_s.shape
    tokens = x.shape[0]
    parts = features // 256
    return pl.pallas_call(
        rotate_grads_kernel,
        out_shape=jax.ShapeDtypeStruct((tokens, features), F32),
        in_specs=[HBM, VMEM],
        out_specs=VMEM,
        scratch_shapes=[pltpu.VMEM((features, depth), BF16), pltpu.SemaphoreType.DMA((parts,))],
        compiler_params=pltpu.CompilerParams(vmem_limit_bytes=52 * MIB),
        cost_estimate=pl.CostEstimate(
            flops=2 * features * depth * 256, bytes_accessed=features * depth * 2, transcendentals=0
        ),
        name="rotate_grads",
    )(eigen_s, x)


def split(x):
    high = x.astype(BF16)
    low = (x - high.astype(F32)).astype(BF16)
    return high, low


def correct_kernel(own_ref, other_ref, a_ref, s1a_ref, s2a_ref, s1g_ref, s2g_ref, o_ref, buffer, g_pairs, sems):
    tokens = own_ref.shape[0]
    n_block, _, width = a_ref.shape
    g_rot = (own_ref[...] + other_ref[...]).astype(BF16)
    product = dot(s1g_ref[...], g_rot) * dot(s2g_ref[...], g_rot) * (1.0 / tokens)
    high, low = split(product)
    g_pairs[...] = jnp.concatenate([high, high, low], axis=0).T
    copies = []
    for block in range(n_block):
        a_rot = a_ref[block]
        high, low = split(dot(s1a_ref[...], a_rot) * dot(s2a_ref[...], a_rot))
        columns = slice(block * width, (block + 1) * width)
        buffer[:, columns] = dot(g_pairs[...], jnp.concatenate([high, low, high], axis=0))
        copies.append(pltpu.make_async_copy(buffer.at[:, columns], o_ref.at[:, columns], sems.at[block]))
        copies[-1].start()
    for copy in copies:
        copy.wait()


def correct(own, other, a_all, s1a, s2a, s1g, s2g):
    tokens, rows = own.shape
    n_row, _, width = a_all.shape
    return pl.pallas_call(
        correct_kernel,
        out_shape=jax.ShapeDtypeStruct((rows, n_row * width), F32),
        in_specs=[VMEM] * 7,
        out_specs=pl.BlockSpec(memory_space=pl.ANY),
        scratch_shapes=[
            pltpu.VMEM((rows, n_row * width), F32),
            pltpu.VMEM((rows, 3 * PAIR_ROWS), BF16),
            pltpu.SemaphoreType.DMA((n_row,)),
        ],
        compiler_params=pltpu.CompilerParams(vmem_limit_bytes=32 * MIB),
        cost_estimate=pl.CostEstimate(
            flops=2 * rows * n_row * width * 256, bytes_accessed=rows * n_row * width * 4, transcendentals=0
        ),
        name="correct",
    )(own, other, a_all, s1a, s2a, s1g, s2g)


def few_tokens_body(acts, grads, eigen_a, eigen_s_rows, doc_lengths, doc_plan):
    n_row = 8
    tokens = n_row * acts.shape[0]
    width = acts.shape[1]

    own = pack(acts, grads)
    beside = lax.ppermute(own, "row", [(i, i ^ 1) for i in range(n_row)])
    both = merge(stage(own), beside)
    pieces = [both] + [
        lax.ppermute(both, "row", [(i, (i + 2 * k) % n_row) for i in range(n_row)]) for k in range(1, 4)
    ]
    basis = load(eigen_a)
    s1a, s2a, s1g, s2g, perm = make_pairs(doc_lengths, doc_plan, tokens)
    acts_own, grads_own = assemble(pieces, basis, perm, width)
    acts_other = lax.ppermute(acts_own, "col", [(0, 1), (1, 0)])
    part = rotate_acts(basis, acts_own)
    copies = rotate_acts(basis, acts_other, part, perm, n_row)
    a_all = lax.all_to_all(copies, "row", 0, 0)
    g_own = rotate_grads(eigen_s_rows, grads_own)
    g_other = lax.ppermute(g_own, "col", [(0, 1), (1, 0)])
    return correct(g_own, g_other, a_all, s1a, s2a, s1g, s2g)


def solution(mesh):
    def body(acts, *rest):
        n_row = mesh.shape["row"]
        tokens = n_row * acts.shape[0]
        most = tokens - (N_SEQ - 1)
        pairs = most * (most + 1) // 2 + N_SEQ - 1
        few = n_row == 8 and acts.shape[0] == 2 and mesh.shape["col"] == 2 and pairs <= PAIR_ROWS
        return (few_tokens_body if few else general_body)(acts, *rest)

    return jax.shard_map(
        body,
        mesh=mesh,
        in_specs=(
            P(("grp", "row"), "col"),
            P(("grp", "row"), "col"),
            P("col", "row", None),
            P("row", "col"),
            P("grp"),
            P("grp"),
        ),
        out_specs=P(("grp", "row"), "col"),
        check_vma=False,
    )
```

```python
import functools
import jax
import jax.numpy as jnp
from jax import lax
from jax.experimental import pallas as pl
from jax.experimental.pallas import tpu as pltpu
from jax.sharding import PartitionSpec as P

N_SEQ = 6
PAIR_ROWS = 80
HEADS = (128, 128)
BF16 = jnp.bfloat16
F32 = jnp.float32
I32 = jnp.int32
NT = (((1,), (1,)), ((), ()))
MIB = 1024 * 1024
HBM = pl.BlockSpec(memory_space=pltpu.HBM)
VMEM = pl.BlockSpec(memory_space=pltpu.VMEM)


def iota(shape, dim):
    return lax.broadcasted_iota(I32, shape, dim)


def dot(a, b, dims=(((1,), (0,)), ((), ()))):
    return lax.dot_general(a, b, dims, preferred_element_type=F32)


def sequence_index(doc_lengths, doc_plan, total_tokens):
    positions = jnp.arange(total_tokens, dtype=I32)
    doc_ends = jnp.cumsum(doc_lengths)
    doc_index = jnp.sum((positions[:, None] >= doc_ends[None, :]).astype(I32), axis=1)
    doc_onehot = (doc_index[:, None] == jnp.arange(doc_lengths.shape[0], dtype=I32)[None, :]).astype(I32)
    return jnp.sum(doc_onehot * doc_plan[None, :], axis=1)


def general_body(acts, grads, eigen_a, eigen_s_rows, doc_lengths, doc_plan):
    act_rows = lax.all_gather(acts, "row", axis=0, tiled=True)
    act_full = lax.all_gather(act_rows, "col", axis=1, tiled=True)
    a_block = dot(eigen_a[0], act_full, NT).astype(BF16)
    a_rot = lax.all_gather(a_block, "row", axis=0, tiled=True)
    grad_terms = dot(eigen_s_rows, lax.all_gather(grads, "row", axis=0, tiled=True), NT)
    g_rot = lax.psum(grad_terms, "col").astype(BF16)
    total_tokens = g_rot.shape[1]
    seq_index = sequence_index(doc_lengths, doc_plan, total_tokens)
    correction = jnp.zeros((g_rot.shape[0], a_rot.shape[0]), F32)
    for sequence in range(N_SEQ):
        inside = (seq_index == sequence).astype(BF16)
        term = dot(g_rot * inside[None, :], a_rot, NT)
        correction = correction + term * term
    return correction / total_tokens


def pairs_kernel(len_ref, plan_ref, s1a_ref, s2a_ref, s1g_ref, s2g_ref, perm_ref):
    docs = len_ref.shape[1]
    tokens = perm_ref.shape[0]
    grid_pairs = tokens * tokens
    me = lax.axis_index("row")
    upper = (iota((docs, docs), 0) <= iota((docs, docs), 1)).astype(F32)
    ends = dot(jnp.broadcast_to(len_ref[...].astype(F32), (8, docs)), upper)[0:1]
    position = iota((tokens, docs), 0).astype(F32)
    doc = jnp.sum((ends <= position).astype(F32), axis=1, keepdims=True)
    onehot = doc == iota((tokens, docs), 1).astype(F32)
    seq = jnp.sum(jnp.where(onehot, plan_ref[...].astype(F32), 0.0), axis=1, keepdims=True)
    p_lane = iota((tokens, grid_pairs), 1)
    t_sub = iota((tokens, grid_pairs), 0)
    first = lax.div(p_lane, tokens)
    second = lax.rem(p_lane, tokens)
    seq_first = jnp.sum(jnp.where(first == t_sub, seq, 0.0), axis=0, keepdims=True)
    seq_second = jnp.sum(jnp.where(second == t_sub, seq, 0.0), axis=0, keepdims=True)
    valid = (seq_first == seq_second) & (first[0:1] <= second[0:1])
    before = (iota((grid_pairs, grid_pairs), 0) < iota((grid_pairs, grid_pairs), 1)).astype(BF16)
    rank = dot(jnp.broadcast_to(valid.astype(F32), (8, grid_pairs)).astype(BF16), before)[0:1]
    place = jnp.where(valid, rank, -1.0)
    pick = (iota((PAIR_ROWS, grid_pairs), 0).astype(F32) == place).astype(BF16)
    p_sub = iota((grid_pairs, tokens), 0)
    t_lane = iota((grid_pairs, tokens), 1)
    is_first = lax.div(p_sub, tokens) == t_lane
    is_second = lax.rem(p_sub, tokens) == t_lane
    factor = jnp.where(lax.div(p_sub, tokens) == lax.rem(p_sub, tokens), 1.0, 2.0)
    s1 = dot(pick, jnp.where(is_first, 1.0, 0.0).astype(BF16)).astype(BF16)
    s1_scaled = dot(pick, jnp.where(is_first, factor, 0.0).astype(BF16)).astype(BF16)
    s2 = dot(pick, jnp.where(is_second, 1.0, 0.0).astype(BF16)).astype(BF16)
    token = iota((tokens, tokens), 0)
    slot = iota((tokens, tokens), 1)
    source = ((me + 8 - 2 * (slot >> 2)) & 7) ^ ((slot >> 1) & 1)
    perm = (token == 2 * source + (slot & 1)).astype(BF16)
    s1a_ref[...] = s1
    s2a_ref[...] = s2
    s1g_ref[...] = dot(s1_scaled, perm).astype(BF16)
    s2g_ref[...] = dot(s2, perm).astype(BF16)
    perm_ref[...] = perm


def make_pairs(doc_lengths, doc_plan, tokens):
    sel = jax.ShapeDtypeStruct((PAIR_ROWS, tokens), BF16)
    return pl.pallas_call(
        pairs_kernel,
        out_shape=(sel, sel, sel, sel, jax.ShapeDtypeStruct((tokens, tokens), BF16)),
        in_specs=[VMEM, VMEM],
        out_specs=(VMEM,) * 5,
        compiler_params=pltpu.CompilerParams(vmem_limit_bytes=2 * MIB),
        cost_estimate=pl.CostEstimate(flops=2_000_000, bytes_accessed=40_000, transcendentals=0),
        name="pairs",
    )(doc_lengths[None, :], doc_plan[None, :])


def pack_kernel(acts_ref, grads_ref, o_ref, sems):
    width = acts_ref.shape[1]
    copies = (
        pltpu.make_async_copy(acts_ref, o_ref.at[:, :width], sems.at[0]),
        pltpu.make_async_copy(grads_ref, o_ref.at[:, width:], sems.at[1]),
    )
    for copy in copies:
        copy.start()
    for copy in copies:
        copy.wait()


def pack(acts, grads):
    rows, width = acts.shape
    return pl.pallas_call(
        pack_kernel,
        out_shape=jax.ShapeDtypeStruct((rows, width + grads.shape[1]), BF16),
        in_specs=[HBM, HBM],
        out_specs=VMEM,
        scratch_shapes=[pltpu.SemaphoreType.DMA((2,))],
        cost_estimate=pl.CostEstimate(flops=0, bytes_accessed=80_000, transcendentals=0),
        name="pack",
    )(acts, grads)


def stage_kernel(own_ref, o_ref):
    o_ref[...] = own_ref[...]


def stage(own):
    return pl.pallas_call(
        stage_kernel,
        out_shape=jax.ShapeDtypeStruct(own.shape, BF16),
        in_specs=[VMEM],
        out_specs=VMEM,
        compiler_params=pltpu.CompilerParams(vmem_limit_bytes=2 * MIB),
        cost_estimate=pl.CostEstimate(flops=10_000, bytes_accessed=2_000_000, transcendentals=0),
        name="stage",
    )(own)


def merge_kernel(own_ref, beside_ref, o_ref):
    o_ref[0] = own_ref[...]
    o_ref[1] = beside_ref[...]


def merge(own, beside):
    return pl.pallas_call(
        merge_kernel,
        out_shape=jax.ShapeDtypeStruct((2,) + own.shape, BF16),
        in_specs=[VMEM] * 2,
        out_specs=VMEM,
        compiler_params=pltpu.CompilerParams(vmem_limit_bytes=2 * MIB),
        cost_estimate=pl.CostEstimate(flops=10_000, bytes_accessed=150_000, transcendentals=0),
        name="merge",
    )(own, beside)


def assemble_kernel(width, p0, p1, p2, p3, basis_ref, perm_ref, acts_ref, grads_ref):
    rows = []
    for piece in (p0, p1, p2, p3):
        for side in range(2):
            rows.append(piece[side].astype(F32))
    whole = jnp.concatenate(rows, axis=0).astype(BF16)
    acts_ref[...] = whole[:, :width]
    grads_ref[...] = whole[:, width:]


def assemble(pieces, basis, perm, width):
    tokens = sum(p.shape[0] * p.shape[1] for p in pieces)
    total = pieces[0].shape[2]
    return pl.pallas_call(
        functools.partial(assemble_kernel, width),
        out_shape=(
            jax.ShapeDtypeStruct((tokens, width), BF16),
            jax.ShapeDtypeStruct((tokens, total - width), BF16),
        ),
        in_specs=[VMEM] * 6,
        out_specs=(VMEM, VMEM),
        compiler_params=pltpu.CompilerParams(vmem_limit_bytes=4 * MIB),
        cost_estimate=pl.CostEstimate(flops=1_000_000, bytes_accessed=600_000, transcendentals=0),
        name="assemble",
    )(*pieces, basis, perm)


def load_kernel(w_ref, o_ref, sem):
    copy = pltpu.make_async_copy(w_ref, o_ref, sem)
    copy.start()
    copy.wait()


def load(w):
    return pl.pallas_call(
        load_kernel,
        out_shape=jax.ShapeDtypeStruct(w.shape, w.dtype),
        in_specs=[HBM],
        out_specs=VMEM,
        scratch_shapes=[pltpu.SemaphoreType.DMA],
        compiler_params=pltpu.CompilerParams(vmem_limit_bytes=42 * MIB),
        cost_estimate=pl.CostEstimate(flops=0, bytes_accessed=w.size * 2, transcendentals=0),
        name="load",
    )(w)


def row_dots(w_ref, x, first, last, columns=slice(None), rows=128):
    return jnp.concatenate([dot(w_ref[i : i + rows, columns], x, NT) for i in range(first, last, rows)], axis=0)


def half_dot(half, w_ref, x_ref):
    depth = x_ref.shape[1]
    columns = pl.ds(pl.multiple_of(half * depth, depth), depth)
    return row_dots(w_ref.at[0], x_ref[...], 0, w_ref.shape[1], columns)


def fetch(s_ref, head_ref, first, sem):
    return pltpu.make_async_copy(s_ref.at[first : first + head_ref.shape[0], :], head_ref, sem)


def rotate_first_kernel(w_ref, x_ref, s_ref, o_ref, head_ref, sem):
    copy = fetch(s_ref, head_ref, 0, sem)
    copy.start()
    o_ref[...] = half_dot(lax.axis_index("col"), w_ref, x_ref)
    copy.wait()


def rotate_second_kernel(w_ref, x_ref, part_ref, perm_ref, s_ref, o_ref, head_ref, sem):
    copy = fetch(s_ref, head_ref, HEADS[0], sem)
    copy.start()
    total = (half_dot(1 - lax.axis_index("col"), w_ref, x_ref) + part_ref[...]).astype(BF16)
    mine = dot(perm_ref[...], total, NT).astype(BF16)
    for row in range(o_ref.shape[0]):
        o_ref[row] = mine
    copy.wait()


def rotate_acts(eigen_a, x, eigen_s, part=None, perm=None, copies=0):
    _, features, _ = eigen_a.shape
    tokens, depth = x.shape
    cost = pl.CostEstimate(
        flops=2 * features * depth * 256, bytes_accessed=features * depth * 2, transcendentals=0
    )
    params = pltpu.CompilerParams(vmem_limit_bytes=34 * MIB)
    scratch = [pltpu.SemaphoreType.DMA]
    if part is None:
        return pl.pallas_call(
            rotate_first_kernel,
            out_shape=(
                jax.ShapeDtypeStruct((features, tokens), F32),
                jax.ShapeDtypeStruct((HEADS[0], eigen_s.shape[1]), BF16),
            ),
            in_specs=[VMEM, VMEM, HBM],
            out_specs=(VMEM, VMEM),
            scratch_shapes=scratch,
            compiler_params=params,
            cost_estimate=cost,
            name="rotate_first",
        )(eigen_a, x, eigen_s)
    return pl.pallas_call(
        rotate_second_kernel,
        out_shape=(
            jax.ShapeDtypeStruct((copies, tokens, features), BF16),
            jax.ShapeDtypeStruct((HEADS[1], eigen_s.shape[1]), BF16),
        ),
        in_specs=[VMEM] * 4 + [HBM],
        out_specs=(VMEM, VMEM),
        scratch_shapes=scratch,
        compiler_params=params,
        cost_estimate=cost,
        name="rotate_second",
    )(eigen_a, x, part, perm, eigen_s)


def rotate_grads_kernel(head0_ref, head1_ref, w_ref, x_ref, o_ref, held, sems):
    first = sum(HEADS)
    parts = sems.shape[0]
    block = held.shape[0] // parts
    spans = [slice(part * block, (part + 1) * block) for part in range(parts)]
    copies = [
        pltpu.make_async_copy(w_ref.at[first + rows.start : first + rows.stop, :], held.at[rows, :], sems.at[part])
        for part, rows in enumerate(spans)
    ]
    for copy in copies:
        copy.start()
    o_ref[:, : HEADS[0]] = row_dots(head0_ref, x_ref[...], 0, HEADS[0]).T
    o_ref[:, HEADS[0] : first] = row_dots(head1_ref, x_ref[...], 0, HEADS[1]).T
    for copy, rows in zip(copies, spans):
        copy.wait()
        o_ref[:, first + rows.start : first + rows.stop] = row_dots(held, x_ref[...], rows.start, rows.stop).T


def rotate_grads(heads, eigen_s, x):
    features, depth = eigen_s.shape
    tokens = x.shape[0]
    rest = features - sum(HEADS)
    parts = rest // 256
    return pl.pallas_call(
        rotate_grads_kernel,
        out_shape=jax.ShapeDtypeStruct((tokens, features), F32),
        in_specs=[VMEM, VMEM, HBM, VMEM],
        out_specs=VMEM,
        scratch_shapes=[pltpu.VMEM((rest, depth), BF16), pltpu.SemaphoreType.DMA((parts,))],
        compiler_params=pltpu.CompilerParams(vmem_limit_bytes=44 * MIB),
        cost_estimate=pl.CostEstimate(
            flops=2 * features * depth * 256, bytes_accessed=features * depth * 2, transcendentals=0
        ),
        name="rotate_grads",
    )(*heads, eigen_s, x)


def split(x):
    high = x.astype(BF16)
    low = (x - high.astype(F32)).astype(BF16)
    return high, low


def correct_kernel(own_ref, other_ref, a_ref, s1a_ref, s2a_ref, s1g_ref, s2g_ref, o_ref, buffer, g_pairs, sems):
    tokens = own_ref.shape[0]
    n_block, _, width = a_ref.shape
    g_rot = (own_ref[...] + other_ref[...]).astype(BF16)
    product = dot(s1g_ref[...], g_rot) * dot(s2g_ref[...], g_rot) * (1.0 / tokens)
    high, low = split(product)
    g_pairs[...] = jnp.concatenate([high, high, low], axis=0).T
    copies = []
    for block in range(n_block):
        a_rot = a_ref[block]
        high, low = split(dot(s1a_ref[...], a_rot) * dot(s2a_ref[...], a_rot))
        columns = slice(block * width, (block + 1) * width)
        buffer[:, columns] = dot(g_pairs[...], jnp.concatenate([high, low, high], axis=0))
        copies.append(pltpu.make_async_copy(buffer.at[:, columns], o_ref.at[:, columns], sems.at[block]))
        copies[-1].start()
    for copy in copies:
        copy.wait()


def correct(own, other, a_all, s1a, s2a, s1g, s2g):
    tokens, rows = own.shape
    n_row, _, width = a_all.shape
    return pl.pallas_call(
        correct_kernel,
        out_shape=jax.ShapeDtypeStruct((rows, n_row * width), F32),
        in_specs=[VMEM] * 7,
        out_specs=pl.BlockSpec(memory_space=pl.ANY),
        scratch_shapes=[
            pltpu.VMEM((rows, n_row * width), F32),
            pltpu.VMEM((rows, 3 * PAIR_ROWS), BF16),
            pltpu.SemaphoreType.DMA((n_row,)),
        ],
        compiler_params=pltpu.CompilerParams(vmem_limit_bytes=32 * MIB),
        cost_estimate=pl.CostEstimate(
            flops=2 * rows * n_row * width * 256, bytes_accessed=rows * n_row * width * 4, transcendentals=0
        ),
        name="correct",
    )(own, other, a_all, s1a, s2a, s1g, s2g)


def few_tokens_body(acts, grads, eigen_a, eigen_s_rows, doc_lengths, doc_plan):
    n_row = 8
    tokens = n_row * acts.shape[0]
    width = acts.shape[1]

    own = pack(acts, grads)
    beside = lax.ppermute(own, "row", [(i, i ^ 1) for i in range(n_row)])
    both = merge(stage(own), beside)
    pieces = [both] + [
        lax.ppermute(both, "row", [(i, (i + 2 * k) % n_row) for i in range(n_row)]) for k in range(1, 4)
    ]
    basis = load(eigen_a)
    s1a, s2a, s1g, s2g, perm = make_pairs(doc_lengths, doc_plan, tokens)
    acts_own, grads_own = assemble(pieces, basis, perm, width)
    acts_other = lax.ppermute(acts_own, "col", [(0, 1), (1, 0)])
    part, head0 = rotate_acts(basis, acts_own, eigen_s_rows)
    copies, head1 = rotate_acts(basis, acts_other, eigen_s_rows, part, perm, n_row)
    a_all = lax.all_to_all(copies, "row", 0, 0)
    g_own = rotate_grads((head0, head1), eigen_s_rows, grads_own)
    g_other = lax.ppermute(g_own, "col", [(0, 1), (1, 0)])
    return correct(g_own, g_other, a_all, s1a, s2a, s1g, s2g)


def solution(mesh):
    def body(acts, *rest):
        n_row = mesh.shape["row"]
        tokens = n_row * acts.shape[0]
        most = tokens - (N_SEQ - 1)
        pairs = most * (most + 1) // 2 + N_SEQ - 1
        rows = rest[2].shape[0]
        few = rows % 256 == 0 and rows > sum(HEADS) and n_row == 8 and acts.shape[0] == 2 and mesh.shape["col"] == 2 and pairs <= PAIR_ROWS
        return (few_tokens_body if few else general_body)(acts, *rest)

    return jax.shard_map(
        body,
        mesh=mesh,
        in_specs=(
            P(("grp", "row"), "col"),
            P(("grp", "row"), "col"),
            P("col", "row", None),
            P("row", "col"),
            P("grp"),
            P("grp"),
        ),
        out_specs=P(("grp", "row"), "col"),
        check_vma=False,
    )
```

```python
import functools
import jax
import jax.numpy as jnp
from jax import lax
from jax.experimental import pallas as pl
from jax.experimental.pallas import tpu as pltpu
from jax.sharding import PartitionSpec as P

N_SEQ = 6
PAIR_ROWS = 80
FIRST = 2
HEADS = (128, 128)
BF16 = jnp.bfloat16
F32 = jnp.float32
I32 = jnp.int32
NT = (((1,), (1,)), ((), ()))
MIB = 1024 * 1024
HBM = pl.BlockSpec(memory_space=pltpu.HBM)
VMEM = pl.BlockSpec(memory_space=pltpu.VMEM)


def iota(shape, dim):
    return lax.broadcasted_iota(I32, shape, dim)


def dot(a, b, dims=(((1,), (0,)), ((), ()))):
    return lax.dot_general(a, b, dims, preferred_element_type=F32)


def sequence_index(doc_lengths, doc_plan, total_tokens):
    positions = jnp.arange(total_tokens, dtype=I32)
    doc_ends = jnp.cumsum(doc_lengths)
    doc_index = jnp.sum((positions[:, None] >= doc_ends[None, :]).astype(I32), axis=1)
    doc_onehot = (doc_index[:, None] == jnp.arange(doc_lengths.shape[0], dtype=I32)[None, :]).astype(I32)
    return jnp.sum(doc_onehot * doc_plan[None, :], axis=1)


def general_body(acts, grads, eigen_a, eigen_s_rows, doc_lengths, doc_plan):
    act_rows = lax.all_gather(acts, "row", axis=0, tiled=True)
    act_full = lax.all_gather(act_rows, "col", axis=1, tiled=True)
    a_block = dot(eigen_a[0], act_full, NT).astype(BF16)
    a_rot = lax.all_gather(a_block, "row", axis=0, tiled=True)
    grad_terms = dot(eigen_s_rows, lax.all_gather(grads, "row", axis=0, tiled=True), NT)
    g_rot = lax.psum(grad_terms, "col").astype(BF16)
    total_tokens = g_rot.shape[1]
    seq_index = sequence_index(doc_lengths, doc_plan, total_tokens)
    correction = jnp.zeros((g_rot.shape[0], a_rot.shape[0]), F32)
    for sequence in range(N_SEQ):
        inside = (seq_index == sequence).astype(BF16)
        term = dot(g_rot * inside[None, :], a_rot, NT)
        correction = correction + term * term
    return correction / total_tokens


def pairs_kernel(len_ref, plan_ref, s1a_ref, s2a_ref, s1g_ref, s2g_ref, perm_ref):
    docs = len_ref.shape[1]
    tokens = perm_ref.shape[0]
    grid_pairs = tokens * tokens
    me = lax.axis_index("row")
    upper = (iota((docs, docs), 0) <= iota((docs, docs), 1)).astype(F32)
    ends = dot(jnp.broadcast_to(len_ref[...].astype(F32), (8, docs)), upper)[0:1]
    position = iota((tokens, docs), 0).astype(F32)
    doc = jnp.sum((ends <= position).astype(F32), axis=1, keepdims=True)
    onehot = doc == iota((tokens, docs), 1).astype(F32)
    seq = jnp.sum(jnp.where(onehot, plan_ref[...].astype(F32), 0.0), axis=1, keepdims=True)
    p_lane = iota((tokens, grid_pairs), 1)
    t_sub = iota((tokens, grid_pairs), 0)
    first = lax.div(p_lane, tokens)
    second = lax.rem(p_lane, tokens)
    seq_first = jnp.sum(jnp.where(first == t_sub, seq, 0.0), axis=0, keepdims=True)
    seq_second = jnp.sum(jnp.where(second == t_sub, seq, 0.0), axis=0, keepdims=True)
    valid = (seq_first == seq_second) & (first[0:1] <= second[0:1])
    before = (iota((grid_pairs, grid_pairs), 0) < iota((grid_pairs, grid_pairs), 1)).astype(BF16)
    rank = dot(jnp.broadcast_to(valid.astype(F32), (8, grid_pairs)).astype(BF16), before)[0:1]
    place = jnp.where(valid, rank, -1.0)
    pick = (iota((PAIR_ROWS, grid_pairs), 0).astype(F32) == place).astype(BF16)
    p_sub = iota((grid_pairs, tokens), 0)
    t_lane = iota((grid_pairs, tokens), 1)
    is_first = lax.div(p_sub, tokens) == t_lane
    is_second = lax.rem(p_sub, tokens) == t_lane
    factor = jnp.where(lax.div(p_sub, tokens) == lax.rem(p_sub, tokens), 1.0, 2.0)
    s1 = dot(pick, jnp.where(is_first, 1.0, 0.0).astype(BF16)).astype(BF16)
    s1_scaled = dot(pick, jnp.where(is_first, factor, 0.0).astype(BF16)).astype(BF16)
    s2 = dot(pick, jnp.where(is_second, 1.0, 0.0).astype(BF16)).astype(BF16)
    token = iota((tokens, tokens), 0)
    slot = iota((tokens, tokens), 1)
    source = ((me + 8 - 2 * (slot >> 2)) & 7) ^ ((slot >> 1) & 1)
    perm = (token == 2 * source + (slot & 1)).astype(BF16)
    s1a_ref[...] = s1
    s2a_ref[...] = s2
    s1g_ref[...] = dot(s1_scaled, perm).astype(BF16)
    s2g_ref[...] = dot(s2, perm).astype(BF16)
    perm_ref[...] = perm


def make_pairs(doc_lengths, doc_plan, tokens):
    sel = jax.ShapeDtypeStruct((PAIR_ROWS, tokens), BF16)
    return pl.pallas_call(
        pairs_kernel,
        out_shape=(sel, sel, sel, sel, jax.ShapeDtypeStruct((tokens, tokens), BF16)),
        in_specs=[VMEM, VMEM],
        out_specs=(VMEM,) * 5,
        compiler_params=pltpu.CompilerParams(vmem_limit_bytes=2 * MIB),
        cost_estimate=pl.CostEstimate(flops=2_000_000, bytes_accessed=40_000, transcendentals=0),
        name="pairs",
    )(doc_lengths[None, :], doc_plan[None, :])


def pack_kernel(acts_ref, grads_ref, o_ref, sems):
    width = acts_ref.shape[1]
    copies = (
        pltpu.make_async_copy(acts_ref, o_ref.at[:, :width], sems.at[0]),
        pltpu.make_async_copy(grads_ref, o_ref.at[:, width:], sems.at[1]),
    )
    for copy in copies:
        copy.start()
    for copy in copies:
        copy.wait()


def pack(acts, grads):
    rows, width = acts.shape
    return pl.pallas_call(
        pack_kernel,
        out_shape=jax.ShapeDtypeStruct((rows, width + grads.shape[1]), BF16),
        in_specs=[HBM, HBM],
        out_specs=VMEM,
        scratch_shapes=[pltpu.SemaphoreType.DMA((2,))],
        cost_estimate=pl.CostEstimate(flops=0, bytes_accessed=80_000, transcendentals=0),
        name="pack",
    )(acts, grads)


def stage_kernel(own_ref, o_ref):
    o_ref[...] = own_ref[...]


def stage(own):
    return pl.pallas_call(
        stage_kernel,
        out_shape=jax.ShapeDtypeStruct(own.shape, BF16),
        in_specs=[VMEM],
        out_specs=VMEM,
        compiler_params=pltpu.CompilerParams(vmem_limit_bytes=2 * MIB),
        cost_estimate=pl.CostEstimate(flops=10_000, bytes_accessed=2_000_000, transcendentals=0),
        name="stage",
    )(own)


def merge_kernel(own_ref, beside_ref, o_ref):
    o_ref[0] = own_ref[...]
    o_ref[1] = beside_ref[...]


def merge(own, beside):
    return pl.pallas_call(
        merge_kernel,
        out_shape=jax.ShapeDtypeStruct((2,) + own.shape, BF16),
        in_specs=[VMEM] * 2,
        out_specs=VMEM,
        compiler_params=pltpu.CompilerParams(vmem_limit_bytes=2 * MIB),
        cost_estimate=pl.CostEstimate(flops=10_000, bytes_accessed=150_000, transcendentals=0),
        name="merge",
    )(own, beside)


def assemble_kernel(width, p0, p1, p2, p3, basis_ref, perm_ref, acts_ref, grads_ref):
    rows = []
    for piece in (p0, p1, p2, p3):
        for side in range(2):
            rows.append(piece[side].astype(F32))
    whole = jnp.concatenate(rows, axis=0).astype(BF16)
    acts_ref[...] = whole[:, :width]
    grads_ref[...] = whole[:, width:]


def assemble(pieces, basis, perm, width):
    tokens = sum(p.shape[0] * p.shape[1] for p in pieces)
    total = pieces[0].shape[2]
    return pl.pallas_call(
        functools.partial(assemble_kernel, width),
        out_shape=(
            jax.ShapeDtypeStruct((tokens, width), BF16),
            jax.ShapeDtypeStruct((tokens, total - width), BF16),
        ),
        in_specs=[VMEM] * 6,
        out_specs=(VMEM, VMEM),
        compiler_params=pltpu.CompilerParams(vmem_limit_bytes=4 * MIB),
        cost_estimate=pl.CostEstimate(flops=1_000_000, bytes_accessed=600_000, transcendentals=0),
        name="assemble",
    )(*pieces, basis, perm)


def load_kernel(w_ref, o_ref, sem):
    copy = pltpu.make_async_copy(w_ref, o_ref, sem)
    copy.start()
    copy.wait()


def load(w):
    return pl.pallas_call(
        load_kernel,
        out_shape=jax.ShapeDtypeStruct(w.shape, w.dtype),
        in_specs=[HBM],
        out_specs=VMEM,
        scratch_shapes=[pltpu.SemaphoreType.DMA],
        compiler_params=pltpu.CompilerParams(vmem_limit_bytes=42 * MIB),
        cost_estimate=pl.CostEstimate(flops=0, bytes_accessed=w.size * 2, transcendentals=0),
        name="load",
    )(w)


def row_dots(w_ref, x, first, last, columns=slice(None), rows=128):
    return jnp.concatenate([dot(w_ref[i : i + rows, columns], x, NT) for i in range(first, last, rows)], axis=0)


def half_dot(half, w_ref, x_ref):
    depth = x_ref.shape[1]
    columns = pl.ds(pl.multiple_of(half * depth, depth), depth)
    return row_dots(w_ref.at[0], x_ref[...], 0, w_ref.shape[1], columns)


def fetch(s_ref, head_ref, first, sem):
    return pltpu.make_async_copy(s_ref.at[first : first + head_ref.shape[0], :], head_ref, sem)


def rotate_first_kernel(w_ref, x_ref, s_ref, o_ref, head_ref, sem):
    copy = fetch(s_ref, head_ref, 0, sem)
    copy.start()
    o_ref[...] = half_dot(lax.axis_index("col"), w_ref, x_ref)
    copy.wait()


def rotate_second_kernel(w_ref, x_ref, part_ref, perm_ref, s_ref, o_ref, head_ref, sem):
    copy = fetch(s_ref, head_ref, HEADS[0], sem)
    copy.start()
    total = (half_dot(1 - lax.axis_index("col"), w_ref, x_ref) + part_ref[...]).astype(BF16)
    mine = dot(perm_ref[...], total, NT).astype(BF16)
    for row in range(o_ref.shape[0]):
        o_ref[row] = mine
    copy.wait()


def rotate_acts(eigen_a, x, eigen_s, part=None, perm=None, copies=0):
    _, features, _ = eigen_a.shape
    tokens, depth = x.shape
    cost = pl.CostEstimate(
        flops=2 * features * depth * 256, bytes_accessed=features * depth * 2, transcendentals=0
    )
    params = pltpu.CompilerParams(vmem_limit_bytes=34 * MIB)
    scratch = [pltpu.SemaphoreType.DMA]
    if part is None:
        return pl.pallas_call(
            rotate_first_kernel,
            out_shape=(
                jax.ShapeDtypeStruct((features, tokens), F32),
                jax.ShapeDtypeStruct((HEADS[0], eigen_s.shape[1]), BF16),
            ),
            in_specs=[VMEM, VMEM, HBM],
            out_specs=(VMEM, VMEM),
            scratch_shapes=scratch,
            compiler_params=params,
            cost_estimate=cost,
            name="rotate_first",
        )(eigen_a, x, eigen_s)
    return pl.pallas_call(
        rotate_second_kernel,
        out_shape=(
            jax.ShapeDtypeStruct((copies, tokens, features), BF16),
            jax.ShapeDtypeStruct((HEADS[1], eigen_s.shape[1]), BF16),
        ),
        in_specs=[VMEM] * 4 + [HBM],
        out_specs=(VMEM, VMEM),
        scratch_shapes=scratch,
        compiler_params=params,
        cost_estimate=cost,
        name="rotate_second",
    )(eigen_a, x, part, perm, eigen_s)


def rotate_grads_kernel(head0_ref, head1_ref, w_ref, x_ref, o_ref, held, sems):
    first = sum(HEADS)
    parts = sems.shape[0]
    block = held.shape[0] // parts
    spans = [slice(part * block, (part + 1) * block) for part in range(parts)]
    copies = [
        pltpu.make_async_copy(w_ref.at[first + rows.start : first + rows.stop, :], held.at[rows, :], sems.at[part])
        for part, rows in enumerate(spans)
    ]
    for copy in copies[:2]:
        copy.start()
    o_ref[:, : HEADS[0]] = row_dots(head0_ref, x_ref[...], 0, HEADS[0]).T
    o_ref[:, HEADS[0] : first] = row_dots(head1_ref, x_ref[...], 0, HEADS[1]).T
    for part, (copy, rows) in enumerate(zip(copies, spans)):
        copy.wait()
        if part + 2 < parts:
            copies[part + 2].start()
        o_ref[:, first + rows.start : first + rows.stop] = row_dots(held, x_ref[...], rows.start, rows.stop).T


def rotate_grads(heads, eigen_s, x):
    features, depth = eigen_s.shape
    tokens = x.shape[0]
    rest = features - sum(HEADS)
    parts = rest // 256
    return pl.pallas_call(
        rotate_grads_kernel,
        out_shape=jax.ShapeDtypeStruct((tokens, features), F32),
        in_specs=[VMEM, VMEM, HBM, VMEM],
        out_specs=VMEM,
        scratch_shapes=[pltpu.VMEM((rest, depth), BF16), pltpu.SemaphoreType.DMA((parts,))],
        compiler_params=pltpu.CompilerParams(vmem_limit_bytes=44 * MIB),
        cost_estimate=pl.CostEstimate(
            flops=2 * features * depth * 256, bytes_accessed=features * depth * 2, transcendentals=0
        ),
        name="rotate_grads",
    )(*heads, eigen_s, x)


def split(x):
    high = x.astype(BF16)
    low = (x - high.astype(F32)).astype(BF16)
    return high, low


def pair_grads_kernel(own_ref, other_ref, s1_ref, s2_ref, o_ref):
    tokens = own_ref.shape[0]
    g_rot = (own_ref[...] + other_ref[...]).astype(BF16)
    product = dot(s1_ref[...], g_rot) * dot(s2_ref[...], g_rot) * (1.0 / tokens)
    high, low = split(product)
    o_ref[...] = jnp.concatenate([high, high, low], axis=0).T


def pair_grads(own, other, s1, s2):
    rows = own.shape[1]
    return pl.pallas_call(
        pair_grads_kernel,
        out_shape=jax.ShapeDtypeStruct((rows, 3 * PAIR_ROWS), BF16),
        in_specs=[VMEM] * 4,
        out_specs=VMEM,
        compiler_params=pltpu.CompilerParams(vmem_limit_bytes=6 * MIB),
        cost_estimate=pl.CostEstimate(flops=2_000_000, bytes_accessed=2_000_000, transcendentals=0),
        name="pair_grads",
    )(own, other, s1, s2)


def correct_kernel(g_ref, a_ref, s1_ref, s2_ref, o_ref, buffer, sems):
    rows = g_ref.shape[0]
    n_block, _, width = a_ref.shape
    step = rows // (sems.shape[0] - n_block + 1)
    copies = []
    for block in range(n_block):
        a_rot = a_ref[block]
        high, low = split(dot(s1_ref[...], a_rot) * dot(s2_ref[...], a_rot))
        a_pairs = jnp.concatenate([high, low, high], axis=0)
        columns = slice(block * width, (block + 1) * width)
        size = step if block == 0 else rows
        for first in range(0, rows, size):
            span = slice(first, first + size)
            buffer[span, columns] = dot(g_ref[span, :], a_pairs)
            copies.append(
                pltpu.make_async_copy(buffer.at[span, columns], o_ref.at[span, columns], sems.at[len(copies)])
            )
            copies[-1].start()
    for copy in copies:
        copy.wait()


def correct(g_pairs, a_all, s1, s2):
    rows = g_pairs.shape[0]
    n_row, _, width = a_all.shape
    return pl.pallas_call(
        correct_kernel,
        out_shape=jax.ShapeDtypeStruct((rows, n_row * width), F32),
        in_specs=[VMEM] * 4,
        out_specs=pl.BlockSpec(memory_space=pl.ANY),
        scratch_shapes=[
            pltpu.VMEM((rows, n_row * width), F32),
            pltpu.SemaphoreType.DMA((n_row + FIRST - 1,)),
        ],
        compiler_params=pltpu.CompilerParams(vmem_limit_bytes=32 * MIB),
        cost_estimate=pl.CostEstimate(
            flops=2 * rows * n_row * width * 256, bytes_accessed=rows * n_row * width * 4, transcendentals=0
        ),
        name="correct",
    )(g_pairs, a_all, s1, s2)


def few_tokens_body(acts, grads, eigen_a, eigen_s_rows, doc_lengths, doc_plan):
    n_row = 8
    tokens = n_row * acts.shape[0]
    width = acts.shape[1]

    own = pack(acts, grads)
    beside = lax.ppermute(own, "row", [(i, i ^ 1) for i in range(n_row)])
    both = merge(stage(own), beside)
    pieces = [both] + [
        lax.ppermute(both, "row", [(i, (i + 2 * k) % n_row) for i in range(n_row)]) for k in range(1, 4)
    ]
    basis = load(eigen_a)
    s1a, s2a, s1g, s2g, perm = make_pairs(doc_lengths, doc_plan, tokens)
    acts_own, grads_own = assemble(pieces, basis, perm, width)
    acts_other = lax.ppermute(acts_own, "col", [(0, 1), (1, 0)])
    part, head0 = rotate_acts(basis, acts_own, eigen_s_rows)
    copies, head1 = rotate_acts(basis, acts_other, eigen_s_rows, part, perm, n_row)
    a_all = lax.all_to_all(copies, "row", 0, 0)
    g_own = rotate_grads((head0, head1), eigen_s_rows, grads_own)
    g_other = lax.ppermute(g_own, "col", [(0, 1), (1, 0)])
    return correct(pair_grads(g_own, g_other, s1g, s2g), a_all, s1a, s2a)


def solution(mesh):
    def body(acts, *rest):
        n_row = mesh.shape["row"]
        tokens = n_row * acts.shape[0]
        most = tokens - (N_SEQ - 1)
        pairs = most * (most + 1) // 2 + N_SEQ - 1
        rows = rest[2].shape[0]
        few = rows % 256 == 0 and rows > sum(HEADS) and n_row == 8 and acts.shape[0] == 2 and mesh.shape["col"] == 2 and pairs <= PAIR_ROWS
        return (few_tokens_body if few else general_body)(acts, *rest)

    return jax.shard_map(
        body,
        mesh=mesh,
        in_specs=(
            P(("grp", "row"), "col"),
            P(("grp", "row"), "col"),
            P("col", "row", None),
            P("row", "col"),
            P("grp"),
            P("grp"),
        ),
        out_specs=P(("grp", "row"), "col"),
        check_vma=False,
    )
```

```python
import functools
import jax
import jax.numpy as jnp
from jax import lax
from jax.experimental import pallas as pl
from jax.experimental.pallas import tpu as pltpu
from jax.sharding import PartitionSpec as P

N_SEQ = 6
PAIR_ROWS = 80
FIRST = 2
HEADS = (128, 128)
BF16 = jnp.bfloat16
F32 = jnp.float32
I32 = jnp.int32
NT = (((1,), (1,)), ((), ()))
MIB = 1024 * 1024
HBM = pl.BlockSpec(memory_space=pltpu.HBM)
VMEM = pl.BlockSpec(memory_space=pltpu.VMEM)


def iota(shape, dim):
    return lax.broadcasted_iota(I32, shape, dim)


def dot(a, b, dims=(((1,), (0,)), ((), ()))):
    return lax.dot_general(a, b, dims, preferred_element_type=F32)


def sequence_index(doc_lengths, doc_plan, total_tokens):
    positions = jnp.arange(total_tokens, dtype=I32)
    doc_ends = jnp.cumsum(doc_lengths)
    doc_index = jnp.sum((positions[:, None] >= doc_ends[None, :]).astype(I32), axis=1)
    doc_onehot = (doc_index[:, None] == jnp.arange(doc_lengths.shape[0], dtype=I32)[None, :]).astype(I32)
    return jnp.sum(doc_onehot * doc_plan[None, :], axis=1)


def general_body(acts, grads, eigen_a, eigen_s_rows, doc_lengths, doc_plan):
    act_rows = lax.all_gather(acts, "row", axis=0, tiled=True)
    act_full = lax.all_gather(act_rows, "col", axis=1, tiled=True)
    a_block = dot(eigen_a[0], act_full, NT).astype(BF16)
    a_rot = lax.all_gather(a_block, "row", axis=0, tiled=True)
    grad_terms = dot(eigen_s_rows, lax.all_gather(grads, "row", axis=0, tiled=True), NT)
    g_rot = lax.psum(grad_terms, "col").astype(BF16)
    total_tokens = g_rot.shape[1]
    seq_index = sequence_index(doc_lengths, doc_plan, total_tokens)
    correction = jnp.zeros((g_rot.shape[0], a_rot.shape[0]), F32)
    for sequence in range(N_SEQ):
        inside = (seq_index == sequence).astype(BF16)
        term = dot(g_rot * inside[None, :], a_rot, NT)
        correction = correction + term * term
    return correction / total_tokens


def pairs_kernel(docs_ref, s1a_ref, s2a_ref, s1g_ref, s2g_ref, perm_ref):
    docs = docs_ref.shape[1]
    lengths, plan = docs_ref[0:1], docs_ref[1:2]
    tokens = perm_ref.shape[0]
    grid_pairs = tokens * tokens
    me = lax.axis_index("row")
    upper = (iota((docs, docs), 0) <= iota((docs, docs), 1)).astype(F32)
    ends = dot(jnp.broadcast_to(lengths.astype(F32), (8, docs)), upper)[0:1]
    position = iota((tokens, docs), 0).astype(F32)
    doc = jnp.sum((ends <= position).astype(F32), axis=1, keepdims=True)
    onehot = doc == iota((tokens, docs), 1).astype(F32)
    seq = jnp.sum(jnp.where(onehot, plan.astype(F32), 0.0), axis=1, keepdims=True)
    p_lane = iota((tokens, grid_pairs), 1)
    t_sub = iota((tokens, grid_pairs), 0)
    first = lax.div(p_lane, tokens)
    second = lax.rem(p_lane, tokens)
    seq_first = jnp.sum(jnp.where(first == t_sub, seq, 0.0), axis=0, keepdims=True)
    seq_second = jnp.sum(jnp.where(second == t_sub, seq, 0.0), axis=0, keepdims=True)
    valid = (seq_first == seq_second) & (first[0:1] <= second[0:1])
    before = (iota((grid_pairs, grid_pairs), 0) < iota((grid_pairs, grid_pairs), 1)).astype(BF16)
    rank = dot(jnp.broadcast_to(valid.astype(F32), (8, grid_pairs)).astype(BF16), before)[0:1]
    place = jnp.where(valid, rank, -1.0)
    pick = (iota((PAIR_ROWS, grid_pairs), 0).astype(F32) == place).astype(BF16)
    p_sub = iota((grid_pairs, tokens), 0)
    t_lane = iota((grid_pairs, tokens), 1)
    is_first = lax.div(p_sub, tokens) == t_lane
    is_second = lax.rem(p_sub, tokens) == t_lane
    factor = jnp.where(lax.div(p_sub, tokens) == lax.rem(p_sub, tokens), 1.0, 2.0)
    s1 = dot(pick, jnp.where(is_first, 1.0, 0.0).astype(BF16)).astype(BF16)
    s1_scaled = dot(pick, jnp.where(is_first, factor, 0.0).astype(BF16)).astype(BF16)
    s2 = dot(pick, jnp.where(is_second, 1.0, 0.0).astype(BF16)).astype(BF16)
    token = iota((tokens, tokens), 0)
    slot = iota((tokens, tokens), 1)
    source = me ^ (2 * (slot >> 2)) ^ ((slot >> 1) & 1)
    perm = (token == 2 * source + (slot & 1)).astype(BF16)
    s1a_ref[...] = s1
    s2a_ref[...] = s2
    s1g_ref[...] = dot(s1_scaled, perm).astype(BF16)
    s2g_ref[...] = dot(s2, perm).astype(BF16)
    perm_ref[...] = perm


def make_pairs(doc_lengths, doc_plan, tokens):
    sel = jax.ShapeDtypeStruct((PAIR_ROWS, tokens), BF16)
    return pl.pallas_call(
        pairs_kernel,
        out_shape=(sel, sel, sel, sel, jax.ShapeDtypeStruct((tokens, tokens), BF16)),
        in_specs=[VMEM],
        out_specs=(VMEM,) * 5,
        compiler_params=pltpu.CompilerParams(vmem_limit_bytes=2 * MIB),
        cost_estimate=pl.CostEstimate(flops=2_000_000, bytes_accessed=40_000, transcendentals=0),
        name="pairs",
    )(jnp.stack([doc_lengths, doc_plan]))


def pack_kernel(acts_ref, grads_ref, o_ref, sems):
    width = acts_ref.shape[1]
    copies = (
        pltpu.make_async_copy(acts_ref, o_ref.at[:, :width], sems.at[0]),
        pltpu.make_async_copy(grads_ref, o_ref.at[:, width:], sems.at[1]),
    )
    for copy in copies:
        copy.start()
    for copy in copies:
        copy.wait()


def pack(acts, grads):
    rows, width = acts.shape
    return pl.pallas_call(
        pack_kernel,
        out_shape=jax.ShapeDtypeStruct((rows, width + grads.shape[1]), BF16),
        in_specs=[HBM, HBM],
        out_specs=VMEM,
        scratch_shapes=[pltpu.SemaphoreType.DMA((2,))],
        cost_estimate=pl.CostEstimate(flops=0, bytes_accessed=2_000_000, transcendentals=0),
        name="pack",
    )(acts, grads)


def stage_kernel(own_ref, o_ref):
    o_ref[...] = own_ref[...]


def stage(own):
    return pl.pallas_call(
        stage_kernel,
        out_shape=jax.ShapeDtypeStruct(own.shape, BF16),
        in_specs=[VMEM],
        out_specs=VMEM,
        compiler_params=pltpu.CompilerParams(vmem_limit_bytes=2 * MIB),
        cost_estimate=pl.CostEstimate(flops=10_000, bytes_accessed=2_000_000, transcendentals=0),
        name="stage",
    )(own)


def merge_kernel(own_ref, beside_ref, perm_ref, o_ref):
    o_ref[0] = own_ref[...]
    o_ref[1] = beside_ref[...]


def merge(own, beside, perm):
    return pl.pallas_call(
        merge_kernel,
        out_shape=jax.ShapeDtypeStruct((2,) + own.shape, BF16),
        in_specs=[VMEM] * 3,
        out_specs=VMEM,
        compiler_params=pltpu.CompilerParams(vmem_limit_bytes=2 * MIB),
        cost_estimate=pl.CostEstimate(flops=10_000, bytes_accessed=150_000, transcendentals=0),
        name="merge",
    )(own, beside, perm)


def assemble_kernel(width, p0, p1, p2, p3, basis_ref, perm_ref, acts_ref, grads_ref):
    rows = []
    for piece in (p0, p1, p2, p3):
        for side in range(2):
            rows.append(piece[side].astype(F32))
    whole = jnp.concatenate(rows, axis=0).astype(BF16)
    acts_ref[...] = whole[:, :width]
    grads_ref[...] = whole[:, width:]


def assemble(pieces, basis, perm, width):
    tokens = sum(p.shape[0] * p.shape[1] for p in pieces)
    total = pieces[0].shape[2]
    return pl.pallas_call(
        functools.partial(assemble_kernel, width),
        out_shape=(
            jax.ShapeDtypeStruct((tokens, width), BF16),
            jax.ShapeDtypeStruct((tokens, total - width), BF16),
        ),
        in_specs=[VMEM] * 6,
        out_specs=(VMEM, VMEM),
        compiler_params=pltpu.CompilerParams(vmem_limit_bytes=4 * MIB),
        cost_estimate=pl.CostEstimate(flops=1_000_000, bytes_accessed=600_000, transcendentals=0),
        name="assemble",
    )(*pieces, basis, perm)


def load_kernel(w_ref, o_ref, sem):
    copy = pltpu.make_async_copy(w_ref, o_ref, sem)
    copy.start()
    copy.wait()


def load(w):
    return pl.pallas_call(
        load_kernel,
        out_shape=jax.ShapeDtypeStruct(w.shape, w.dtype),
        in_specs=[HBM],
        out_specs=VMEM,
        scratch_shapes=[pltpu.SemaphoreType.DMA],
        compiler_params=pltpu.CompilerParams(vmem_limit_bytes=42 * MIB),
        cost_estimate=pl.CostEstimate(flops=0, bytes_accessed=w.size * 2, transcendentals=0),
        name="load",
    )(w)


def row_dots(w_ref, x, first, last, columns=slice(None), rows=128):
    return jnp.concatenate([dot(w_ref[i : i + rows, columns], x, NT) for i in range(first, last, rows)], axis=0)


def half_dot(half, w_ref, x_ref):
    depth = x_ref.shape[1]
    columns = pl.ds(pl.multiple_of(half * depth, depth), depth)
    return row_dots(w_ref.at[0], x_ref[...], 0, w_ref.shape[1], columns)


def fetch(s_ref, head_ref, first, sem):
    return pltpu.make_async_copy(s_ref.at[first : first + head_ref.shape[0], :], head_ref, sem)


def rotate_first_kernel(w_ref, x_ref, s_ref, o_ref, head_ref, sem):
    copy = fetch(s_ref, head_ref, 0, sem)
    copy.start()
    o_ref[...] = half_dot(lax.axis_index("col"), w_ref, x_ref)
    copy.wait()


def rotate_second_kernel(w_ref, x_ref, part_ref, perm_ref, s_ref, o_ref, head_ref, sem):
    copy = fetch(s_ref, head_ref, HEADS[0], sem)
    copy.start()
    total = (half_dot(1 - lax.axis_index("col"), w_ref, x_ref) + part_ref[...]).astype(BF16)
    mine = dot(perm_ref[...], total, NT).astype(BF16)
    for row in range(o_ref.shape[0]):
        o_ref[row] = mine
    copy.wait()


def rotate_acts(eigen_a, x, eigen_s, part=None, perm=None, copies=0):
    _, features, _ = eigen_a.shape
    tokens, depth = x.shape
    cost = pl.CostEstimate(
        flops=2 * features * depth * 256, bytes_accessed=features * depth * 2, transcendentals=0
    )
    params = pltpu.CompilerParams(vmem_limit_bytes=34 * MIB)
    scratch = [pltpu.SemaphoreType.DMA]
    if part is None:
        return pl.pallas_call(
            rotate_first_kernel,
            out_shape=(
                jax.ShapeDtypeStruct((features, tokens), F32),
                jax.ShapeDtypeStruct((HEADS[0], eigen_s.shape[1]), BF16),
            ),
            in_specs=[VMEM, VMEM, HBM],
            out_specs=(VMEM, VMEM),
            scratch_shapes=scratch,
            compiler_params=params,
            cost_estimate=cost,
            name="rotate_first",
        )(eigen_a, x, eigen_s)
    return pl.pallas_call(
        rotate_second_kernel,
        out_shape=(
            jax.ShapeDtypeStruct((copies, tokens, features), BF16),
            jax.ShapeDtypeStruct((HEADS[1], eigen_s.shape[1]), BF16),
        ),
        in_specs=[VMEM] * 4 + [HBM],
        out_specs=(VMEM, VMEM),
        scratch_shapes=scratch,
        compiler_params=params,
        cost_estimate=cost,
        name="rotate_second",
    )(eigen_a, x, part, perm, eigen_s)


def rotate_grads_kernel(head0_ref, head1_ref, w_ref, x_ref, o_ref, held, sems):
    first = sum(HEADS)
    parts = sems.shape[0]
    block = held.shape[0] // parts
    spans = [slice(part * block, (part + 1) * block) for part in range(parts)]
    copies = [
        pltpu.make_async_copy(w_ref.at[first + rows.start : first + rows.stop, :], held.at[rows, :], sems.at[part])
        for part, rows in enumerate(spans)
    ]
    for copy in copies[:2]:
        copy.start()
    o_ref[:, : HEADS[0]] = row_dots(head0_ref, x_ref[...], 0, HEADS[0]).T
    o_ref[:, HEADS[0] : first] = row_dots(head1_ref, x_ref[...], 0, HEADS[1]).T
    for part, (copy, rows) in enumerate(zip(copies, spans)):
        copy.wait()
        if part + 2 < parts:
            copies[part + 2].start()
        o_ref[:, first + rows.start : first + rows.stop] = row_dots(held, x_ref[...], rows.start, rows.stop).T


def rotate_grads(heads, eigen_s, x):
    features, depth = eigen_s.shape
    tokens = x.shape[0]
    rest = features - sum(HEADS)
    parts = rest // 256
    return pl.pallas_call(
        rotate_grads_kernel,
        out_shape=jax.ShapeDtypeStruct((tokens, features), F32),
        in_specs=[VMEM, VMEM, HBM, VMEM],
        out_specs=VMEM,
        scratch_shapes=[pltpu.VMEM((rest, depth), BF16), pltpu.SemaphoreType.DMA((parts,))],
        compiler_params=pltpu.CompilerParams(vmem_limit_bytes=44 * MIB),
        cost_estimate=pl.CostEstimate(
            flops=2 * features * depth * 256, bytes_accessed=features * depth * 2, transcendentals=0
        ),
        name="rotate_grads",
    )(*heads, eigen_s, x)


def split(x):
    high = x.astype(BF16)
    low = (x - high.astype(F32)).astype(BF16)
    return high, low


def pair_grads_kernel(own_ref, other_ref, s1_ref, s2_ref, o_ref):
    tokens = own_ref.shape[0]
    g_rot = (own_ref[...] + other_ref[...]).astype(BF16)
    product = dot(s1_ref[...], g_rot) * dot(s2_ref[...], g_rot) * (1.0 / tokens)
    high, low = split(product)
    o_ref[...] = jnp.concatenate([high, high, low], axis=0).T


def pair_grads(own, other, s1, s2):
    rows = own.shape[1]
    return pl.pallas_call(
        pair_grads_kernel,
        out_shape=jax.ShapeDtypeStruct((rows, 3 * PAIR_ROWS), BF16),
        in_specs=[VMEM] * 4,
        out_specs=VMEM,
        compiler_params=pltpu.CompilerParams(vmem_limit_bytes=6 * MIB),
        cost_estimate=pl.CostEstimate(flops=2_000_000, bytes_accessed=2_000_000, transcendentals=0),
        name="pair_grads",
    )(own, other, s1, s2)


def correct_kernel(g_ref, a_ref, s1_ref, s2_ref, o_ref, buffer, sems):
    rows = g_ref.shape[0]
    n_block, _, width = a_ref.shape
    step = rows // (sems.shape[0] - n_block + 1)
    copies = []
    for block in range(n_block):
        a_rot = a_ref[block]
        high, low = split(dot(s1_ref[...], a_rot) * dot(s2_ref[...], a_rot))
        a_pairs = jnp.concatenate([high, low, high], axis=0)
        columns = slice(block * width, (block + 1) * width)
        size = step if block == 0 else rows
        for first in range(0, rows, size):
            span = slice(first, first + size)
            buffer[span, columns] = dot(g_ref[span, :], a_pairs)
            copies.append(
                pltpu.make_async_copy(buffer.at[span, columns], o_ref.at[span, columns], sems.at[len(copies)])
            )
            copies[-1].start()
    for copy in copies:
        copy.wait()


def correct(g_pairs, a_all, s1, s2):
    rows = g_pairs.shape[0]
    n_row, _, width = a_all.shape
    return pl.pallas_call(
        correct_kernel,
        out_shape=jax.ShapeDtypeStruct((rows, n_row * width), F32),
        in_specs=[VMEM] * 4,
        out_specs=pl.BlockSpec(memory_space=pl.ANY),
        scratch_shapes=[
            pltpu.VMEM((rows, n_row * width), F32),
            pltpu.SemaphoreType.DMA((n_row + FIRST - 1,)),
        ],
        compiler_params=pltpu.CompilerParams(vmem_limit_bytes=32 * MIB),
        cost_estimate=pl.CostEstimate(
            flops=2 * rows * n_row * width * 256, bytes_accessed=rows * n_row * width * 4, transcendentals=0
        ),
        name="correct",
    )(g_pairs, a_all, s1, s2)


def few_tokens_body(acts, grads, eigen_a, eigen_s_rows, doc_lengths, doc_plan):
    n_row = 8
    tokens = n_row * acts.shape[0]
    width = acts.shape[1]

    s1a, s2a, s1g, s2g, perm = make_pairs(doc_lengths, doc_plan, tokens)
    own = pack(acts, grads)
    beside = lax.ppermute(own, "row", [(i, i ^ 1) for i in range(n_row)])
    both = merge(stage(own), beside, perm)
    pieces = [both] + [
        lax.ppermute(both, "row", [(i, i ^ (2 * k)) for i in range(n_row)]) for k in range(1, 4)
    ]
    basis = load(eigen_a)
    acts_own, grads_own = assemble(pieces, basis, perm, width)
    acts_other = lax.ppermute(acts_own, "col", [(0, 1), (1, 0)])
    part, head0 = rotate_acts(basis, acts_own, eigen_s_rows)
    copies, head1 = rotate_acts(basis, acts_other, eigen_s_rows, part, perm, n_row)
    a_all = lax.all_to_all(copies, "row", 0, 0)
    g_own = rotate_grads((head0, head1), eigen_s_rows, grads_own)
    g_other = lax.ppermute(g_own, "col", [(0, 1), (1, 0)])
    return correct(pair_grads(g_own, g_other, s1g, s2g), a_all, s1a, s2a)


def solution(mesh):
    def body(acts, *rest):
        n_row = mesh.shape["row"]
        tokens = n_row * acts.shape[0]
        most = tokens - (N_SEQ - 1)
        pairs = most * (most + 1) // 2 + N_SEQ - 1
        rows = rest[2].shape[0]
        few = rows % 256 == 0 and rows > sum(HEADS) and n_row == 8 and acts.shape[0] == 2 and mesh.shape["col"] == 2 and pairs <= PAIR_ROWS
        return (few_tokens_body if few else general_body)(acts, *rest)

    return jax.shard_map(
        body,
        mesh=mesh,
        in_specs=(
            P(("grp", "row"), "col"),
            P(("grp", "row"), "col"),
            P("col", "row", None),
            P("row", "col"),
            P("grp"),
            P("grp"),
        ),
        out_specs=P(("grp", "row"), "col"),
        check_vma=False,
    )
```

```python
import functools
import jax
import jax.numpy as jnp
from jax import lax
from jax.experimental import pallas as pl
from jax.experimental.pallas import tpu as pltpu
from jax.sharding import PartitionSpec as P

N_SEQ = 6
PAIR_ROWS = 80
FIRST = 2
HEADS = (128, 128)
BF16 = jnp.bfloat16
F32 = jnp.float32
I32 = jnp.int32
NT = (((1,), (1,)), ((), ()))
MIB = 1024 * 1024
HBM = pl.BlockSpec(memory_space=pltpu.HBM)
VMEM = pl.BlockSpec(memory_space=pltpu.VMEM)


def iota(shape, dim):
    return lax.broadcasted_iota(I32, shape, dim)


def dot(a, b, dims=(((1,), (0,)), ((), ()))):
    return lax.dot_general(a, b, dims, preferred_element_type=F32)


def sequence_index(doc_lengths, doc_plan, total_tokens):
    positions = jnp.arange(total_tokens, dtype=I32)
    doc_ends = jnp.cumsum(doc_lengths)
    doc_index = jnp.sum((positions[:, None] >= doc_ends[None, :]).astype(I32), axis=1)
    doc_onehot = (doc_index[:, None] == jnp.arange(doc_lengths.shape[0], dtype=I32)[None, :]).astype(I32)
    return jnp.sum(doc_onehot * doc_plan[None, :], axis=1)


def general_body(acts, grads, eigen_a, eigen_s_rows, doc_lengths, doc_plan):
    act_rows = lax.all_gather(acts, "row", axis=0, tiled=True)
    act_full = lax.all_gather(act_rows, "col", axis=1, tiled=True)
    a_block = dot(eigen_a[0], act_full, NT).astype(BF16)
    a_rot = lax.all_gather(a_block, "row", axis=0, tiled=True)
    grad_terms = dot(eigen_s_rows, lax.all_gather(grads, "row", axis=0, tiled=True), NT)
    g_rot = lax.psum(grad_terms, "col").astype(BF16)
    total_tokens = g_rot.shape[1]
    seq_index = sequence_index(doc_lengths, doc_plan, total_tokens)
    correction = jnp.zeros((g_rot.shape[0], a_rot.shape[0]), F32)
    for sequence in range(N_SEQ):
        inside = (seq_index == sequence).astype(BF16)
        term = dot(g_rot * inside[None, :], a_rot, NT)
        correction = correction + term * term
    return correction / total_tokens


def pairs_kernel(docs_ref, s1a_ref, s2a_ref, s1g_ref, s2g_ref, perm_ref):
    docs = docs_ref.shape[1]
    lengths, plan = docs_ref[0:1], docs_ref[1:2]
    tokens = perm_ref.shape[0]
    grid_pairs = tokens * tokens
    me = lax.axis_index("row")
    upper = (iota((docs, docs), 0) <= iota((docs, docs), 1)).astype(F32)
    ends = dot(jnp.broadcast_to(lengths.astype(F32), (8, docs)), upper)[0:1]
    position = iota((tokens, docs), 0).astype(F32)
    doc = jnp.sum((ends <= position).astype(F32), axis=1, keepdims=True)
    onehot = doc == iota((tokens, docs), 1).astype(F32)
    seq = jnp.sum(jnp.where(onehot, plan.astype(F32), 0.0), axis=1, keepdims=True)
    p_lane = iota((tokens, grid_pairs), 1)
    t_sub = iota((tokens, grid_pairs), 0)
    first = lax.div(p_lane, tokens)
    second = lax.rem(p_lane, tokens)
    seq_first = jnp.sum(jnp.where(first == t_sub, seq, 0.0), axis=0, keepdims=True)
    seq_second = jnp.sum(jnp.where(second == t_sub, seq, 0.0), axis=0, keepdims=True)
    valid = (seq_first == seq_second) & (first[0:1] <= second[0:1])
    before = (iota((grid_pairs, grid_pairs), 0) < iota((grid_pairs, grid_pairs), 1)).astype(BF16)
    rank = dot(jnp.broadcast_to(valid.astype(F32), (8, grid_pairs)).astype(BF16), before)[0:1]
    place = jnp.where(valid, rank, -1.0)
    pick = (iota((PAIR_ROWS, grid_pairs), 0).astype(F32) == place).astype(BF16)
    p_sub = iota((grid_pairs, tokens), 0)
    t_lane = iota((grid_pairs, tokens), 1)
    is_first = lax.div(p_sub, tokens) == t_lane
    is_second = lax.rem(p_sub, tokens) == t_lane
    factor = jnp.where(lax.div(p_sub, tokens) == lax.rem(p_sub, tokens), 1.0, 2.0)
    s1 = dot(pick, jnp.where(is_first, 1.0, 0.0).astype(BF16)).astype(BF16)
    s1_scaled = dot(pick, jnp.where(is_first, factor, 0.0).astype(BF16)).astype(BF16)
    s2 = dot(pick, jnp.where(is_second, 1.0, 0.0).astype(BF16)).astype(BF16)
    token = iota((tokens, tokens), 0)
    slot = iota((tokens, tokens), 1)
    source = me ^ (2 * (slot >> 2)) ^ ((slot >> 1) & 1)
    perm = (token == 2 * source + (slot & 1)).astype(BF16)
    s1a_ref[...] = s1
    s2a_ref[...] = s2
    s1g_ref[...] = dot(s1_scaled, perm).astype(BF16)
    s2g_ref[...] = dot(s2, perm).astype(BF16)
    perm_ref[...] = perm


def make_pairs(doc_lengths, doc_plan, tokens):
    sel = jax.ShapeDtypeStruct((PAIR_ROWS, tokens), BF16)
    return pl.pallas_call(
        pairs_kernel,
        out_shape=(sel, sel, sel, sel, jax.ShapeDtypeStruct((tokens, tokens), BF16)),
        in_specs=[VMEM],
        out_specs=(VMEM,) * 5,
        compiler_params=pltpu.CompilerParams(vmem_limit_bytes=2 * MIB),
        cost_estimate=pl.CostEstimate(flops=2_000_000, bytes_accessed=40_000, transcendentals=0),
        name="pairs",
    )(jnp.stack([doc_lengths, doc_plan]))


def merge_kernel(own_ref, beside_ref, perm_ref, o_ref):
    o_ref[0] = own_ref[...]
    o_ref[1] = beside_ref[...]


def merge(own, beside, perm):
    return pl.pallas_call(
        merge_kernel,
        out_shape=jax.ShapeDtypeStruct((2,) + own.shape, BF16),
        in_specs=[VMEM] * 3,
        out_specs=VMEM,
        compiler_params=pltpu.CompilerParams(vmem_limit_bytes=2 * MIB),
        cost_estimate=pl.CostEstimate(flops=10_000, bytes_accessed=150_000, transcendentals=0),
        name="merge",
    )(own, beside, perm)


def assemble_kernel(width, p0, p1, p2, p3, basis_ref, perm_ref, acts_ref, grads_ref):
    rows = []
    for piece in (p0, p1, p2, p3):
        for side in range(2):
            rows.append(piece[side].astype(F32))
    whole = jnp.concatenate(rows, axis=0).astype(BF16)
    acts_ref[...] = whole[:, :width]
    grads_ref[...] = whole[:, width:]


def assemble(pieces, basis, perm, width):
    tokens = sum(p.shape[0] * p.shape[1] for p in pieces)
    total = pieces[0].shape[2]
    return pl.pallas_call(
        functools.partial(assemble_kernel, width),
        out_shape=(
            jax.ShapeDtypeStruct((tokens, width), BF16),
            jax.ShapeDtypeStruct((tokens, total - width), BF16),
        ),
        in_specs=[VMEM] * 6,
        out_specs=(VMEM, VMEM),
        compiler_params=pltpu.CompilerParams(vmem_limit_bytes=4 * MIB),
        cost_estimate=pl.CostEstimate(flops=1_000_000, bytes_accessed=600_000, transcendentals=0),
        name="assemble",
    )(*pieces, basis, perm)


def load_kernel(w_ref, o_ref, sem):
    copy = pltpu.make_async_copy(w_ref, o_ref, sem)
    copy.start()
    copy.wait()


def load(w):
    return pl.pallas_call(
        load_kernel,
        out_shape=jax.ShapeDtypeStruct(w.shape, w.dtype),
        in_specs=[HBM],
        out_specs=VMEM,
        scratch_shapes=[pltpu.SemaphoreType.DMA],
        compiler_params=pltpu.CompilerParams(vmem_limit_bytes=42 * MIB),
        cost_estimate=pl.CostEstimate(flops=0, bytes_accessed=w.size * 2, transcendentals=0),
        name="load",
    )(w)


def row_dots(w_ref, x, first, last, columns=slice(None), rows=128):
    return jnp.concatenate([dot(w_ref[i : i + rows, columns], x, NT) for i in range(first, last, rows)], axis=0)


def half_dot(half, w_ref, x_ref):
    depth = x_ref.shape[1]
    columns = pl.ds(pl.multiple_of(half * depth, depth), depth)
    return row_dots(w_ref.at[0], x_ref[...], 0, w_ref.shape[1], columns)


def fetch(s_ref, head_ref, first, sem):
    return pltpu.make_async_copy(s_ref.at[first : first + head_ref.shape[0], :], head_ref, sem)


def rotate_first_kernel(w_ref, x_ref, s_ref, o_ref, head_ref, sem):
    copy = fetch(s_ref, head_ref, 0, sem)
    copy.start()
    o_ref[...] = half_dot(lax.axis_index("col"), w_ref, x_ref)
    copy.wait()


def rotate_second_kernel(w_ref, x_ref, part_ref, perm_ref, s_ref, o_ref, head_ref, sem):
    copy = fetch(s_ref, head_ref, HEADS[0], sem)
    copy.start()
    total = (half_dot(1 - lax.axis_index("col"), w_ref, x_ref) + part_ref[...]).astype(BF16)
    mine = dot(perm_ref[...], total, NT).astype(BF16)
    for row in range(o_ref.shape[0]):
        o_ref[row] = mine
    copy.wait()


def rotate_acts(eigen_a, x, eigen_s, part=None, perm=None, copies=0):
    _, features, _ = eigen_a.shape
    tokens, depth = x.shape
    cost = pl.CostEstimate(
        flops=2 * features * depth * 256, bytes_accessed=features * depth * 2, transcendentals=0
    )
    params = pltpu.CompilerParams(vmem_limit_bytes=34 * MIB)
    scratch = [pltpu.SemaphoreType.DMA]
    if part is None:
        return pl.pallas_call(
            rotate_first_kernel,
            out_shape=(
                jax.ShapeDtypeStruct((features, tokens), F32),
                jax.ShapeDtypeStruct((HEADS[0], eigen_s.shape[1]), BF16),
            ),
            in_specs=[VMEM, VMEM, HBM],
            out_specs=(VMEM, VMEM),
            scratch_shapes=scratch,
            compiler_params=params,
            cost_estimate=cost,
            name="rotate_first",
        )(eigen_a, x, eigen_s)
    return pl.pallas_call(
        rotate_second_kernel,
        out_shape=(
            jax.ShapeDtypeStruct((copies, tokens, features), BF16),
            jax.ShapeDtypeStruct((HEADS[1], eigen_s.shape[1]), BF16),
        ),
        in_specs=[VMEM] * 4 + [HBM],
        out_specs=(VMEM, VMEM),
        scratch_shapes=scratch,
        compiler_params=params,
        cost_estimate=cost,
        name="rotate_second",
    )(eigen_a, x, part, perm, eigen_s)


def rotate_grads_kernel(head0_ref, head1_ref, w_ref, x_ref, o_ref, held, sems):
    first = sum(HEADS)
    parts = sems.shape[0]
    block = held.shape[0] // parts
    spans = [slice(part * block, (part + 1) * block) for part in range(parts)]
    copies = [
        pltpu.make_async_copy(w_ref.at[first + rows.start : first + rows.stop, :], held.at[rows, :], sems.at[part])
        for part, rows in enumerate(spans)
    ]
    for copy in copies[:2]:
        copy.start()
    o_ref[:, : HEADS[0]] = row_dots(head0_ref, x_ref[...], 0, HEADS[0]).T
    o_ref[:, HEADS[0] : first] = row_dots(head1_ref, x_ref[...], 0, HEADS[1]).T
    for part, (copy, rows) in enumerate(zip(copies, spans)):
        copy.wait()
        if part + 2 < parts:
            copies[part + 2].start()
        o_ref[:, first + rows.start : first + rows.stop] = row_dots(held, x_ref[...], rows.start, rows.stop).T


def rotate_grads(heads, eigen_s, x):
    features, depth = eigen_s.shape
    tokens = x.shape[0]
    rest = features - sum(HEADS)
    parts = rest // 256
    return pl.pallas_call(
        rotate_grads_kernel,
        out_shape=jax.ShapeDtypeStruct((tokens, features), F32),
        in_specs=[VMEM, VMEM, HBM, VMEM],
        out_specs=VMEM,
        scratch_shapes=[pltpu.VMEM((rest, depth), BF16), pltpu.SemaphoreType.DMA((parts,))],
        compiler_params=pltpu.CompilerParams(vmem_limit_bytes=44 * MIB),
        cost_estimate=pl.CostEstimate(
            flops=2 * features * depth * 256, bytes_accessed=features * depth * 2, transcendentals=0
        ),
        name="rotate_grads",
    )(*heads, eigen_s, x)


def split(x):
    high = x.astype(BF16)
    low = (x - high.astype(F32)).astype(BF16)
    return high, low


def pair_grads_kernel(own_ref, other_ref, s1_ref, s2_ref, o_ref):
    tokens = own_ref.shape[0]
    g_rot = (own_ref[...] + other_ref[...]).astype(BF16)
    product = dot(s1_ref[...], g_rot) * dot(s2_ref[...], g_rot) * (1.0 / tokens)
    high, low = split(product)
    o_ref[...] = jnp.concatenate([high, high, low], axis=0).T


def pair_grads(own, other, s1, s2):
    rows = own.shape[1]
    return pl.pallas_call(
        pair_grads_kernel,
        out_shape=jax.ShapeDtypeStruct((rows, 3 * PAIR_ROWS), BF16),
        in_specs=[VMEM] * 4,
        out_specs=VMEM,
        compiler_params=pltpu.CompilerParams(vmem_limit_bytes=6 * MIB),
        cost_estimate=pl.CostEstimate(flops=2_000_000, bytes_accessed=2_000_000, transcendentals=0),
        name="pair_grads",
    )(own, other, s1, s2)


def correct_kernel(g_ref, a_ref, s1_ref, s2_ref, o_ref, buffer, sems):
    rows = g_ref.shape[0]
    n_block, _, width = a_ref.shape
    step = rows // (sems.shape[0] - n_block + 1)
    copies = []
    for block in range(n_block):
        a_rot = a_ref[block]
        high, low = split(dot(s1_ref[...], a_rot) * dot(s2_ref[...], a_rot))
        a_pairs = jnp.concatenate([high, low, high], axis=0)
        columns = slice(block * width, (block + 1) * width)
        size = step if block == 0 else rows
        for first in range(0, rows, size):
            span = slice(first, first + size)
            buffer[span, columns] = dot(g_ref[span, :], a_pairs)
            copies.append(
                pltpu.make_async_copy(buffer.at[span, columns], o_ref.at[span, columns], sems.at[len(copies)])
            )
            copies[-1].start()
    for copy in copies:
        copy.wait()


def correct(g_pairs, a_all, s1, s2):
    rows = g_pairs.shape[0]
    n_row, _, width = a_all.shape
    return pl.pallas_call(
        correct_kernel,
        out_shape=jax.ShapeDtypeStruct((rows, n_row * width), F32),
        in_specs=[VMEM] * 4,
        out_specs=pl.BlockSpec(memory_space=pl.ANY),
        scratch_shapes=[
            pltpu.VMEM((rows, n_row * width), F32),
            pltpu.SemaphoreType.DMA((n_row + FIRST - 1,)),
        ],
        compiler_params=pltpu.CompilerParams(vmem_limit_bytes=32 * MIB),
        cost_estimate=pl.CostEstimate(
            flops=2 * rows * n_row * width * 256, bytes_accessed=rows * n_row * width * 4, transcendentals=0
        ),
        name="correct",
    )(g_pairs, a_all, s1, s2)


def few_tokens_body(acts, grads, eigen_a, eigen_s_rows, doc_lengths, doc_plan):
    n_row = 8
    tokens = n_row * acts.shape[0]
    width = acts.shape[1]

    s1a, s2a, s1g, s2g, perm = make_pairs(doc_lengths, doc_plan, tokens)
    own = jnp.concatenate([acts, grads], axis=1)
    beside = lax.ppermute(own, "row", [(i, i ^ 1) for i in range(n_row)])
    both = merge(own, beside, perm)
    pieces = [both] + [
        lax.ppermute(both, "row", [(i, i ^ (2 * k)) for i in range(n_row)]) for k in range(1, 4)
    ]
    basis = load(eigen_a)
    acts_own, grads_own = assemble(pieces, basis, perm, width)
    acts_other = lax.ppermute(acts_own, "col", [(0, 1), (1, 0)])
    part, head0 = rotate_acts(basis, acts_own, eigen_s_rows)
    copies, head1 = rotate_acts(basis, acts_other, eigen_s_rows, part, perm, n_row)
    a_all = lax.all_to_all(copies, "row", 0, 0)
    g_own = rotate_grads((head0, head1), eigen_s_rows, grads_own)
    g_other = lax.ppermute(g_own, "col", [(0, 1), (1, 0)])
    return correct(pair_grads(g_own, g_other, s1g, s2g), a_all, s1a, s2a)


def solution(mesh):
    def body(acts, *rest):
        n_row = mesh.shape["row"]
        tokens = n_row * acts.shape[0]
        most = tokens - (N_SEQ - 1)
        pairs = most * (most + 1) // 2 + N_SEQ - 1
        rows = rest[2].shape[0]
        few = rows % 256 == 0 and rows > sum(HEADS) and n_row == 8 and acts.shape[0] == 2 and mesh.shape["col"] == 2 and pairs <= PAIR_ROWS
        return (few_tokens_body if few else general_body)(acts, *rest)

    return jax.shard_map(
        body,
        mesh=mesh,
        in_specs=(
            P(("grp", "row"), "col"),
            P(("grp", "row"), "col"),
            P("col", "row", None),
            P("row", "col"),
            P("grp"),
            P("grp"),
        ),
        out_specs=P(("grp", "row"), "col"),
        check_vma=False,
    )
```
